256 devices in a mesh: mem: 16 (over x_lo, y, core), lon: 16 (over z, x_hi).
Axes of the slice: x: 4 (x_hi: 2, x_lo: 2; x = x_hi * 2 + x_lo), y: 4, z: 8, core: 2. Of those that a mesh axis runs over, the one named last changes fastest.
Arguments:
- members: bfloat16 [32, 32, 32, 2048], P('mem', None, None, 'lon'), may hold values from -6 to 6
- conv_one: bfloat16 [32, 32, 5, 5], replicated, may hold values from -0.21875 to 0.21875
- conv_two: bfloat16 [32, 32, 5, 5], replicated, may hold values from -0.21875 to 0.21875
- conv_three: bfloat16 [32, 32, 5, 5], replicated, may hold values from -0.21875 to 0.21875
- norm_gain: float32 [32], replicated, may hold values from 0.1 to 1.9
- w_query: bfloat16 [32, 32], replicated, may hold values from -9 to 9
- w_key: bfloat16 [32, 32], replicated, may hold values from -1 to 1
- w_value: bfloat16 [32, 32], replicated, may hold values from -1 to 1
- w_out: bfloat16 [32, 32], replicated, may hold values from -1 to 1
Outputs:
- ensemble_out: bfloat16 [32, 32, 32, 2048], P('mem', None, None, 'lon')
The draws below stay inside these ranges and needn't reach their ends.
All inputs are finite; a program needn't handle non-finite values.
Results may differ from the reference program's by a relative error of at most 0.03.
Values may be sent and summed in bfloat16 or wider, within the bound.
A program may use at most 64 MiB of HBM per device.

```python
import jax
import jax.numpy as jnp
from jax import lax

C = 32
HEADS = 4
M = 32
LAT = 32
LON = 2048


def draw_w_query(key, part):
    key = jax.random.fold_in(key, 1)
    base = jnp.clip(jax.random.normal(key, (C, C), jnp.float32), -4.0, 4.0) * C ** (-0.5)
    return base.astype(jnp.bfloat16)


def block_scale(own_key, extent, shards, least, largest):
    def one(dim, shards_of):
        heights = jax.random.uniform(jax.random.fold_in(jax.random.fold_in(own_key, 6), dim), (shards_of,), jnp.float32, least / len(shards), largest / len(shards))
        return jnp.repeat(jnp.exp(heights), extent[dim] // shards_of).reshape((-1,) + (1,) * (len(extent) - dim - 1))

    level = one(*shards[0])
    for cut in shards[1:]:
        level = level * one(*cut)
    return level


def normal_values(stream_key, extent, scale, limit, cuts=(), kind=jnp.bfloat16):
    array = scale * jax.random.normal(stream_key, extent, jnp.float32)
    if cuts:
        array = array * block_scale(stream_key, extent, cuts, -0.22, 0.18)
    return jnp.clip(array, -limit, limit).astype(kind)


def setup_inputs(seed: int = 0) -> dict:
    key_list = jax.random.split(jax.random.key(seed), 10)
    return {
        "members": normal_values(key_list[0], (M, C, LAT, LON), 1.0, 6.0, ((0, 16), (3, 16))),
        "conv_one": normal_values(key_list[1], (C, C, 5, 5), (C * 25) ** -0.5, 0.21875),
        "conv_two": normal_values(key_list[2], (C, C, 5, 5), (C * 25) ** -0.5, 0.21875),
        "conv_three": normal_values(key_list[3], (C, C, 5, 5), (C * 25) ** -0.5, 0.21875),
        "norm_gain": jnp.clip(1.0 + 0.18 * jax.random.normal(key_list[4], (C,), jnp.float32), 0.1, 1.9),
        "w_query": draw_w_query(jax.random.fold_in(key_list[9], 71), 0),
        "w_key": normal_values(key_list[6], (C, C), C ** -0.5, 1.0),
        "w_value": normal_values(key_list[7], (C, C), C ** -0.5, 1.0),
        "w_out": normal_values(key_list[8], (C, C), C ** -0.5, 1.0),
    }


def convolve(padded, kernel):
    return lax.conv_general_dilated(padded, kernel, (1, 1), ((2, 2), (0, 0)), dimension_numbers=('NCHW', 'OIHW', 'NCHW'), preferred_element_type=jnp.float32)

def wrap_pad(field, width):
    return jnp.concatenate([field[..., -width:], field, field[..., :width]], axis=-1)

def member_stack(member, conv_one, conv_two, conv_three):
    batch = member[None]
    first = jax.nn.silu(convolve(wrap_pad(batch, 2), conv_one)).astype(jnp.bfloat16)
    second = jax.nn.silu(convolve(wrap_pad(first, 2), conv_two)).astype(jnp.bfloat16)
    third = convolve(wrap_pad(second, 2), conv_three)
    return (batch.astype(jnp.float32) + third).astype(jnp.bfloat16)[0]

def normalize(state, gain):
    values = state.astype(jnp.float32)
    centre = lax.optimization_barrier(jnp.mean(values, axis=1, keepdims=True))
    centred = values - centre
    spread = lax.optimization_barrier(jnp.mean(centred * centred, axis=1, keepdims=True))
    return (centred * lax.rsqrt(spread + 1e-05) * gain[None, :, None, None]).astype(jnp.bfloat16)

def project(state, weight):
    return jnp.einsum('dc,mdyx->mcyx', weight.astype(jnp.float32), state.astype(jnp.float32))

def attend(query, keys, values, heads):
    size = query.shape[1] // heads
    pieces = []
    for head in range(heads):
        low = head * size
        high = low + size
        scores = jnp.einsum('mdyx,ndyx->mnyx', query[:, low:high].astype(jnp.float32), keys[:, low:high].astype(jnp.float32)) / jnp.sqrt(jnp.float32(size))
        peak = lax.optimization_barrier(jnp.max(scores, axis=1, keepdims=True))
        weights = jnp.exp(scores - peak)
        probs = (weights / lax.optimization_barrier(jnp.sum(weights, axis=1, keepdims=True))).astype(jnp.bfloat16)
        pieces.append(jnp.einsum('mnyx,ndyx->mdyx', probs.astype(jnp.float32), values[:, low:high].astype(jnp.float32)))
    return jnp.concatenate(pieces, axis=1).astype(jnp.bfloat16)

def reference(members, conv_one, conv_two, conv_three, norm_gain, w_query, w_key, w_value, w_out):
    state_all = lax.map(lambda member: member_stack(member, conv_one, conv_two, conv_three), members)

    def row_out(index):
        state = lax.dynamic_slice_in_dim(state_all, index, 1, 2)
        normed = normalize(state, norm_gain)
        query = project(normed, w_query).astype(jnp.bfloat16)
        keys = project(normed, w_key).astype(jnp.bfloat16)
        values = project(normed, w_value).astype(jnp.bfloat16)
        mixed = attend(query, keys, values, HEADS)
        final = (state.astype(jnp.float32) + project(mixed, w_out)).astype(jnp.bfloat16)
        return final[:, :, 0, :]
    rows = lax.map(row_out, jnp.arange(LAT, dtype=jnp.int32))
    return jnp.transpose(rows, (1, 2, 0, 3))
```

```python
import math

import jax
import jax.numpy as jnp
from jax import lax
from jax.experimental import pallas as pl
from jax.experimental.pallas import tpu as pltpu
from jax.sharding import PartitionSpec as P

MESH = pl.DeviceIdType.MESH
HEADS = 4
BF = jnp.bfloat16
F32 = jnp.float32
PEERS = 16


def iota(shape, dim):
    return lax.broadcasted_iota(jnp.int32, shape, dim)


def ones_where(mask):
    return jnp.where(mask, 1.0, 0.0).astype(BF)


def dot(a, b, contract=((1,), (0,))):
    return lax.dot_general(a, b, (contract, ((), ())), preferred_element_type=F32)


def device(**where):
    return {name: index for name, index in where.items()}


def kernel(
    x_ref,
    w1_ref,
    w2_ref,
    w3_ref,
    gain_ref,
    wq_ref,
    wk_ref,
    wv_ref,
    wo_ref,
    out_ref,
    z_ref,
    xa_ref,
    xb_ref,
    xc_ref,
    band_ref,
    proj_ref,
    back_ref,
    gcol_ref,
    hs_ref,
    hr_ref,
    send_ref,
    recv_ref,
    q_ref,
    k_ref,
    v_ref,
    s_ref,
    mix_ref,
    ret_ref,
    got_ref,
    halo_send,
    halo_recv,
    go_send,
    go_recv,
    back_send,
    back_recv,
):
    me = lax.axis_index("mem")
    col = lax.axis_index("lon")
    right, left = lax.rem(col + 1, PEERS), lax.rem(col + PEERS - 1, PEERS)

    barrier = pltpu.get_barrier_semaphore()

    def greet(step, carry):
        pl.semaphore_signal(
            barrier, inc=1, device_id={"mem": lax.rem(me + step, PEERS)}, device_id_type=MESH
        )
        return carry

    for side in (left, right):
        pl.semaphore_signal(barrier, inc=1, device_id={"lon": side}, device_id_type=MESH)
    lax.fori_loop(1, PEERS, greet, 0)

    for m in range(2):
        z_ref[m] = x_ref[m].astype(F32).reshape(1024, 128)
    for buf in (xa_ref, xb_ref, xc_ref):
        buf[0:64, :] = jnp.zeros((64, 384), BF)
        buf[1088:1152, :] = jnp.zeros((64, 384), BF)
    for m in range(2):
        for lat in range(32):
            rows = z_ref[m, pl.ds(lat, 32, stride=32), :]
            xa_ref[64 + 32 * lat : 96 + 32 * lat, 128 * m : 128 * m + 128] = rows.astype(BF)

    r, lane = iota((32, 256), 0), iota((32, 256), 1)
    want = jnp.where(r < 16, 0, 120) + (r & 7) + jnp.where((r & 8) != 0, 128, 0)
    edges = dot(ones_where(lane == want), xa_ref[64:1088, 0:256], ((1,), (1,)))
    edges = edges.astype(BF)
    hs_ref[0] = edges[0:16]
    hs_ref[1] = edges[16:32]

    pl.semaphore_wait(barrier, PEERS + 1)

    def halo(side, target):
        return pltpu.make_async_remote_copy(
            src_ref=hs_ref.at[side],
            dst_ref=hr_ref.at[side],
            send_sem=halo_send.at[side],
            recv_sem=halo_recv.at[side],
            device_id={"lon": target},
            device_id_type=MESH,
        )

    to_left, to_right = halo(0, left), halo(1, right)
    to_left.start()
    to_right.start()

    for layer, w_ref in enumerate((w1_ref, w2_ref, w3_ref)):
        for dx in range(5):
            pieces = [w_ref[dy, dx].astype(F32) for dy in range(5)]
            base = jnp.concatenate(pieces + [jnp.zeros((32, 96), F32)], axis=1)
            for up in range(4):
                rolled = base if up == 0 else pltpu.roll(base, 32 * up, 1)
                at = dx * 128 + up * 32
                band_ref[layer, at : at + 32, :] = rolled.astype(BF)

    r, c = iota((256, 32), 0), iota((256, 32), 1)
    spread = ones_where((r >> 3) == c)
    spread_out = ones_where((r & 31) == c)
    c, lane = iota((32, 256), 0), iota((32, 256), 1)
    tile = ones_where((lane & 31) == c)
    tile_out = ones_where((lane >> 3) == c)
    r, lane = iota((256, 256), 0), iota((256, 256), 1)
    own = (r & 7) == (lane >> 5)
    own_out = (r >> 5) == (lane & 7)
    for index, w_ref in enumerate((wq_ref, wk_ref, wv_ref)):
        tall = dot(spread, w_ref[...], ((1,), (1,))).astype(BF)
        full = jnp.where(own, dot(tall, tile), 0.0)
        proj_ref[256 * index : 256 * index + 256, :] = full.astype(BF)
    tall = dot(spread_out, wo_ref[...], ((1,), (1,))).astype(BF)
    back_ref[...] = jnp.where(own_out, dot(tall, tile_out), 0.0).astype(BF)
    eye = iota((32, 32), 0) == iota((32, 32), 1)
    gains = jnp.broadcast_to(gain_ref[...], (32, 32))
    gcol = jnp.sum(jnp.where(eye, gains, 0.0), axis=1, keepdims=True)
    gcol_ref[...] = jnp.broadcast_to(gcol, (32, 128))

    to_left.wait()
    to_right.wait()

    r, lane = iota((256, 128), 0), iota((256, 128), 1)
    lon, base = r & 127, (r >> 7) * 64
    inner = jnp.where(lon < 16, base + 16 + lon, jnp.where(lon >= 112, base + lon - 80, -1))
    r2, lane2 = iota((32, 128), 0), iota((32, 128), 1)
    outer = jnp.where(r2 < 16, 48, 8) + (r2 & 7) + jnp.where((r2 & 8) != 0, 64, 0)
    strip = dot(xa_ref[64:1088, 0:256], ones_where(lane == inner))
    ring = hr_ref[...].reshape(32, 1024)
    strip = strip + dot(ring, ones_where(lane2 == outer), ((0,), (0,)))
    xa_ref[64:1088, 256:384] = strip.astype(BF)

    def convolve(source, layer, block):
        window = source[pl.ds(pl.multiple_of(block * 128, 128), 256), :]
        total = [None, None, None]
        for dx in range(5):
            y = dot(band_ref[layer, dx * 128 : dx * 128 + 128, :], window)
            for t in range(3):
                part = y[:, 128 * t : 128 * t + 128]
                if dx != 2:
                    part = pltpu.roll(part, (2 - dx) % 128, 1)
                total[t] = part if total[t] is None else total[t] + part
        return total

    def silu_layer(source, target, layer):
        def body(block, carry):
            total = convolve(source, layer, block)
            at = pl.ds(pl.multiple_of(64 + block * 128, 64), 128)
            for t in range(3):
                value = 0.5 * total[t]
                value = value * jnp.tanh(value) + value
                target[at, 128 * t : 128 * t + 128] = value.astype(BF)
            return carry

        lax.fori_loop(0, 8, body, 0)

    silu_layer(xa_ref, xb_ref, 0)
    silu_layer(xb_ref, xc_ref, 1)

    def go(slot, peer):
        return pltpu.make_async_remote_copy(
            src_ref=send_ref.at[16 * slot + peer],
            dst_ref=recv_ref.at[slot, me],
            send_sem=go_send.at[slot, peer],
            recv_sem=go_recv.at[slot, me],
            device_id={"mem": peer},
            device_id_type=MESH,
        )

    def last_layer(step, carry):
        slot = step // 4
        quarter = lax.rem(step + me // 4, 4)
        block = slot * 4 + quarter
        total = convolve(xc_ref, 2, block)
        at = pl.ds(pl.multiple_of(64 + block * 128, 64), 128)
        state = []
        for t in range(3):
            value = total[t] + xa_ref[at, 128 * t : 128 * t + 128].astype(F32)
            state.append(value.astype(BF).astype(F32))
        lane = iota((128, 128), 1)
        for m in range(2):
            low = pltpu.roll(state[2], 112 - 64 * m, 1)
            high = pltpu.roll(state[2], (80 - 64 * m) % 128, 1)
            whole = jnp.where(lane < 8, low, jnp.where(lane >= 120, high, state[m]))
            whole = whole.astype(BF)
            for row in range(4):
                send_ref[4 * block + row, m] = whole[32 * row : 32 * row + 32]
        for row in range(4):
            peer = quarter * 4 + row

            @pl.when(peer != me)
            def _():
                go(slot, peer).start()

            @pl.when(peer == me)
            def _():
                recv_ref[slot, me] = send_ref[16 * slot + me]

        return carry

    lax.fori_loop(0, 8, last_layer, 0)

    scale = math.log2(math.e) / math.sqrt(32 // HEADS)

    def back(slot, peer):
        return pltpu.make_async_remote_copy(
            src_ref=ret_ref.at[slot, peer],
            dst_ref=got_ref.at[16 * slot + me],
            send_sem=back_send.at[slot, peer],
            recv_sem=back_recv.at[slot, me],
            device_id={"mem": peer},
            device_id_type=MESH,
        )

    def attend(slot, carry):
        def arrived(step, carry):
            peer = lax.rem(me + step, PEERS)
            pltpu.make_async_remote_copy(
                src_ref=send_ref.at[16 * slot + peer],
                dst_ref=recv_ref.at[slot, peer],
                send_sem=go_send.at[slot, peer],
                recv_sem=go_recv.at[slot, peer],
                device_id={"mem": peer},
                device_id_type=MESH,
            ).wait_recv()
            return carry

        lax.fori_loop(1, PEERS, arrived, 0)

        def prepare(group, carry):
            values = recv_ref[slot, pl.ds(4 * group, 4)].astype(F32).reshape(8, 32, 128)
            centred = values - jnp.mean(values, axis=1, keepdims=True)
            spread = jnp.mean(centred * centred, axis=1, keepdims=True)
            normed = centred * lax.rsqrt(spread + 1e-05) * gcol_ref[...][None]
            out = dot(proj_ref[...], normed.astype(BF).reshape(256, 128))
            out = out.astype(BF).astype(F32)
            q_ref[group] = (out[0:256] * scale).reshape(32, 8, 128)
            k_ref[group] = out[256:512].reshape(32, 8, 128)
            v_ref[group] = out[512:768].reshape(32, 8, 128)
            return carry

        lax.fori_loop(0, 4, prepare, 0)

        def head(h, carry):
            queries = [[q_ref[mb, 8 * h + d] for mb in range(4)] for d in range(8)]

            def score(group, peak):
                peak = list(peak)
                for n in range(8):
                    total = [None] * 4
                    for d in range(8):
                        key = jnp.broadcast_to(k_ref[group, 8 * h + d, n : n + 1, :], (8, 128))
                        for mb in range(4):
                            term = queries[d][mb] * key
                            total[mb] = term if d == 0 else total[mb] + term
                    for mb in range(4):
                        s_ref[8 * group + n, mb] = total[mb]
                        peak[mb] = jnp.maximum(peak[mb], total[mb])
                return tuple(peak)

            low = jnp.full((8, 128), -jnp.inf, F32)
            peak = lax.fori_loop(0, 4, score, (low,) * 4)

            def mix(group, state):
                weight, mixed = list(state[0]), [list(m) for m in state[1]]
                for n in range(8):
                    probs = [jnp.exp2(s_ref[8 * group + n, mb] - peak[mb]) for mb in range(4)]
                    for mb in range(4):
                        weight[mb] = weight[mb] + probs[mb]
                    for d in range(8):
                        value = jnp.broadcast_to(v_ref[group, 8 * h + d, n : n + 1, :], (8, 128))
                        for mb in range(4):
                            mixed[d][mb] = mixed[d][mb] + probs[mb] * value
                return tuple(weight), tuple(tuple(m) for m in mixed)

            zero = jnp.zeros((8, 128), F32)
            weight, mixed = lax.fori_loop(0, 4, mix, ((zero,) * 4, ((zero,) * 4,) * 8))
            for mb in range(4):
                inverse = 1.0 / weight[mb]
                for d in range(8):
                    mix_ref[mb, 8 * h + d] = mixed[d][mb] * inverse
            return carry

        lax.fori_loop(0, HEADS, head, 0)

        def finish(group, carry):
            mixed = mix_ref[group].reshape(256, 128).astype(BF)
            state = recv_ref[slot, pl.ds(4 * group, 4)].astype(F32).reshape(256, 128)
            final = dot(back_ref[...], mixed) + state
            ret_ref[slot, pl.ds(4 * group, 4)] = final.astype(BF).reshape(4, 2, 32, 128)
            for row in range(4):
                peer = 4 * group + row

                @pl.when(peer != me)
                def _():
                    back(slot, peer).start()

                @pl.when(peer == me)
                def _():
                    got_ref[16 * slot + me] = ret_ref[slot, me]

            return carry

        lax.fori_loop(0, 4, finish, 0)
        return carry

    lax.fori_loop(0, 2, attend, 0)

    def returned(slot, carry):
        def one(step, carry):
            peer = lax.rem(me + step, PEERS)
            pltpu.make_async_remote_copy(
                src_ref=ret_ref.at[slot, peer],
                dst_ref=got_ref.at[16 * slot + peer],
                send_sem=back_send.at[slot, peer],
                recv_sem=back_recv.at[slot, peer],
                device_id={"mem": peer},
                device_id_type=MESH,
            ).wait_recv()
            return carry

        lax.fori_loop(1, PEERS, one, 0)

        def place(lat, carry):
            for m in range(2):
                z_ref[m, pl.ds(16 * slot + lat, 32, stride=32), :] = got_ref[
                    16 * slot + lat, m
                ].astype(F32)
            return carry

        lax.fori_loop(0, 16, place, 0)
        return carry

    lax.fori_loop(0, 2, returned, 0)
    for m in range(2):
        out_ref[m] = z_ref[m].astype(BF).reshape(32, 32, 128)

    def sent(step, carry):
        peer = lax.rem(me + step, PEERS)
        for slot in range(2):
            go(slot, peer).wait_send()
            back(slot, peer).wait_send()
        return carry

    lax.fori_loop(1, PEERS, sent, 0)


def on_device(members, conv_one, conv_two, conv_three, norm_gain, w_query, w_key, w_value, w_out):
    taps = [jnp.transpose(w, (2, 3, 0, 1)) for w in (conv_one, conv_two, conv_three)]
    vmem = pl.BlockSpec(memory_space=pltpu.VMEM)
    return pl.pallas_call(
        kernel,
        out_shape=jax.ShapeDtypeStruct(members.shape, BF),
        in_specs=[vmem] * 9,
        out_specs=vmem,
        scratch_shapes=[
            pltpu.VMEM((2, 1024, 128), F32),
            pltpu.VMEM((1152, 384), BF),
            pltpu.VMEM((1152, 384), BF),
            pltpu.VMEM((1152, 384), BF),
            pltpu.VMEM((3, 640, 256), BF),
            pltpu.VMEM((768, 256), BF),
            pltpu.VMEM((256, 256), BF),
            pltpu.VMEM((32, 128), F32),
            pltpu.VMEM((2, 16, 1024), BF),
            pltpu.VMEM((2, 16, 1024), BF),
            pltpu.VMEM((32, 2, 32, 128), BF),
            pltpu.VMEM((2, 16, 2, 32, 128), BF),
            pltpu.VMEM((4, 32, 8, 128), F32),
            pltpu.VMEM((4, 32, 8, 128), F32),
            pltpu.VMEM((4, 32, 8, 128), F32),
            pltpu.VMEM((32, 4, 8, 128), F32),
            pltpu.VMEM((4, 32, 8, 128), F32),
            pltpu.VMEM((2, 16, 2, 32, 128), BF),
            pltpu.VMEM((32, 2, 32, 128), BF),
            pltpu.SemaphoreType.DMA((2,)),
            pltpu.SemaphoreType.DMA((2,)),
            pltpu.SemaphoreType.DMA((2, 16)),
            pltpu.SemaphoreType.DMA((2, 16)),
            pltpu.SemaphoreType.DMA((2, 16)),
            pltpu.SemaphoreType.DMA((2, 16)),
        ],
        compiler_params=pltpu.CompilerParams(
            collective_id=0, has_side_effects=True, vmem_limit_bytes=40 * 1024 * 1024
        ),
    )(members, *taps, norm_gain.reshape(1, 32), w_query, w_key, w_value, w_out)


def solution(mesh):
    in_specs = (P("mem", None, None, "lon"), P(), P(), P(), P(), P(), P(), P(), P())
    out_specs = P("mem", None, None, "lon")
    return jax.shard_map(
        on_device, mesh=mesh, in_specs=in_specs, out_specs=out_specs, check_vma=False
    )
```

```python
import math

import jax
import jax.numpy as jnp
from jax import lax
from jax.experimental import pallas as pl
from jax.experimental.pallas import tpu as pltpu
from jax.sharding import PartitionSpec as P

MESH = pl.DeviceIdType.MESH
HEADS = 4
BF = jnp.bfloat16
F32 = jnp.float32
PEERS = 16


def iota(shape, dim):
    return lax.broadcasted_iota(jnp.int32, shape, dim)


def ones_where(mask):
    return jnp.where(mask, 1.0, 0.0).astype(BF)


def dot(a, b, contract=((1,), (0,))):
    return lax.dot_general(a, b, (contract, ((), ())), preferred_element_type=F32)


def device(**where):
    return {name: index for name, index in where.items()}


def kernel(
    x_hbm,
    w1_hbm,
    w2_hbm,
    w3_hbm,
    gain_hbm,
    wq_hbm,
    wk_hbm,
    wv_hbm,
    wo_hbm,
    out_ref,
    x_ref,
    w1_ref,
    w2_ref,
    w3_ref,
    gain_ref,
    wq_ref,
    wk_ref,
    wv_ref,
    wo_ref,
    z_ref,
    xa_ref,
    xb_ref,
    xc_ref,
    band_ref,
    proj_ref,
    back_ref,
    gcol_ref,
    hs_ref,
    hr_ref,
    send_ref,
    recv_ref,
    q_ref,
    k_ref,
    v_ref,
    s_ref,
    mix_ref,
    ret_ref,
    got_ref,
    halo_send,
    halo_recv,
    go_send,
    go_recv,
    back_send,
    back_recv,
    load_sem,
):
    loads = [
        pltpu.make_async_copy(source, target, load_sem.at[index])
        for index, (source, target) in enumerate(
            (
                (x_hbm, x_ref),
                (w1_hbm, w1_ref),
                (w2_hbm, w2_ref),
                (w3_hbm, w3_ref),
                (gain_hbm, gain_ref),
                (wq_hbm, wq_ref),
                (wk_hbm, wk_ref),
                (wv_hbm, wv_ref),
                (wo_hbm, wo_ref),
            )
        )
    ]
    for load in loads:
        load.start()
    me = lax.axis_index("mem")
    col = lax.axis_index("lon")
    right, left = lax.rem(col + 1, PEERS), lax.rem(col + PEERS - 1, PEERS)

    barrier = pltpu.get_barrier_semaphore()

    def greet(step, carry):
        pl.semaphore_signal(
            barrier, inc=1, device_id={"mem": lax.rem(me + step, PEERS)}, device_id_type=MESH
        )
        return carry

    for side in (left, right):
        pl.semaphore_signal(barrier, inc=1, device_id={"lon": side}, device_id_type=MESH)
    lax.fori_loop(1, PEERS, greet, 0)

    for buf in (xa_ref, xb_ref, xc_ref):
        buf[0:64, :] = jnp.zeros((64, 384), BF)
        buf[1088:1152, :] = jnp.zeros((64, 384), BF)
    loads[0].wait()
    for m in range(2):
        z_ref[m] = x_ref[m].astype(F32).reshape(1024, 128)
        for lat in range(32):
            rows = z_ref[m, pl.ds(lat, 32, stride=32), :]
            xa_ref[64 + 32 * lat : 96 + 32 * lat, 128 * m : 128 * m + 128] = rows.astype(BF)

    r, lane = iota((32, 256), 0), iota((32, 256), 1)
    want = jnp.where(r < 16, 0, 120) + (r & 7) + jnp.where((r & 8) != 0, 128, 0)
    edges = dot(ones_where(lane == want), xa_ref[64:1088, 0:256], ((1,), (1,)))
    edges = edges.astype(BF)
    hs_ref[0] = edges[0:16]
    hs_ref[1] = edges[16:32]

    pl.semaphore_wait(barrier, PEERS + 1)

    def halo(side, target):
        return pltpu.make_async_remote_copy(
            src_ref=hs_ref.at[side],
            dst_ref=hr_ref.at[side],
            send_sem=halo_send.at[side],
            recv_sem=halo_recv.at[side],
            device_id={"lon": target},
            device_id_type=MESH,
        )

    to_left, to_right = halo(0, left), halo(1, right)
    to_left.start()
    to_right.start()

    for load in loads[1:]:
        load.wait()

    for layer, w_ref in enumerate((w1_ref, w2_ref, w3_ref)):
        for dx in range(5):
            pieces = [w_ref[dy, dx].astype(F32) for dy in range(5)]
            base = jnp.concatenate(pieces + [jnp.zeros((32, 96), F32)], axis=1)
            for up in range(4):
                rolled = base if up == 0 else pltpu.roll(base, 32 * up, 1)
                at = dx * 128 + up * 32
                band_ref[layer, at : at + 32, :] = rolled.astype(BF)

    r, c = iota((256, 32), 0), iota((256, 32), 1)
    spread = ones_where((r >> 3) == c)
    spread_out = ones_where((r & 31) == c)
    c, lane = iota((32, 256), 0), iota((32, 256), 1)
    tile = ones_where((lane & 31) == c)
    tile_out = ones_where((lane >> 3) == c)
    r, lane = iota((256, 256), 0), iota((256, 256), 1)
    own = (r & 7) == (lane >> 5)
    own_out = (r >> 5) == (lane & 7)
    for index, w_ref in enumerate((wq_ref, wk_ref, wv_ref)):
        tall = dot(spread, w_ref[...], ((1,), (1,))).astype(BF)
        full = jnp.where(own, dot(tall, tile), 0.0)
        proj_ref[256 * index : 256 * index + 256, :] = full.astype(BF)
    tall = dot(spread_out, wo_ref[...], ((1,), (1,))).astype(BF)
    back_ref[...] = jnp.where(own_out, dot(tall, tile_out), 0.0).astype(BF)
    eye = iota((32, 32), 0) == iota((32, 32), 1)
    gains = jnp.broadcast_to(gain_ref[...], (32, 32))
    gcol = jnp.sum(jnp.where(eye, gains, 0.0), axis=1, keepdims=True)
    gcol_ref[...] = jnp.broadcast_to(gcol, (32, 128))

    to_left.wait()
    to_right.wait()

    r, lane = iota((256, 128), 0), iota((256, 128), 1)
    lon, base = r & 127, (r >> 7) * 64
    inner = jnp.where(lon < 16, base + 16 + lon, jnp.where(lon >= 112, base + lon - 80, -1))
    r2, lane2 = iota((32, 128), 0), iota((32, 128), 1)
    outer = jnp.where(r2 < 16, 48, 8) + (r2 & 7) + jnp.where((r2 & 8) != 0, 64, 0)
    strip = dot(xa_ref[64:1088, 0:256], ones_where(lane == inner))
    ring = hr_ref[...].reshape(32, 1024)
    strip = strip + dot(ring, ones_where(lane2 == outer), ((0,), (0,)))
    xa_ref[64:1088, 256:384] = strip.astype(BF)

    def convolve(source, layer, block):
        window = source[pl.ds(pl.multiple_of(block * 128, 128), 256), :]
        total = [None, None, None]
        for dx in range(5):
            y = dot(band_ref[layer, dx * 128 : dx * 128 + 128, :], window)
            for t in range(3):
                part = y[:, 128 * t : 128 * t + 128]
                if dx != 2:
                    part = pltpu.roll(part, (2 - dx) % 128, 1)
                total[t] = part if total[t] is None else total[t] + part
        return total

    def silu_layer(source, target, layer):
        def body(block, carry):
            total = convolve(source, layer, block)
            at = pl.ds(pl.multiple_of(64 + block * 128, 64), 128)
            for t in range(3):
                value = 0.5 * total[t]
                value = value * jnp.tanh(value) + value
                target[at, 128 * t : 128 * t + 128] = value.astype(BF)
            return carry

        lax.fori_loop(0, 8, body, 0, unroll=8)

    silu_layer(xa_ref, xb_ref, 0)
    silu_layer(xb_ref, xc_ref, 1)

    def go(slot, peer):
        return pltpu.make_async_remote_copy(
            src_ref=send_ref.at[16 * slot + peer],
            dst_ref=recv_ref.at[slot, me],
            send_sem=go_send.at[slot, peer],
            recv_sem=go_recv.at[slot, me],
            device_id={"mem": peer},
            device_id_type=MESH,
        )

    def last_layer(slot, carry):
        for step in range(4):
            quarter = lax.rem(step + me // 4, 4)
            block = slot * 4 + quarter
            total = convolve(xc_ref, 2, block)
            at = pl.ds(pl.multiple_of(64 + block * 128, 64), 128)
            state = []
            for t in range(3):
                value = total[t] + xa_ref[at, 128 * t : 128 * t + 128].astype(F32)
                state.append(value.astype(BF).astype(F32))
            lane = iota((128, 128), 1)
            for m in range(2):
                low = pltpu.roll(state[2], 112 - 64 * m, 1)
                high = pltpu.roll(state[2], (80 - 64 * m) % 128, 1)
                whole = jnp.where(lane < 8, low, jnp.where(lane >= 120, high, state[m]))
                whole = whole.astype(BF)
                for row in range(4):
                    send_ref[4 * block + row, m] = whole[32 * row : 32 * row + 32]
            if step == 0:
                recv_ref[slot, me] = send_ref[16 * slot + me]
            for row in range(1 if step == 0 else 0, 4):
                go(slot, quarter * 4 + lax.rem(me + row, 4)).start()
        return carry

    lax.fori_loop(0, 2, last_layer, 0)

    scale = math.log2(math.e) / math.sqrt(32 // HEADS)

    def back(slot, peer):
        return pltpu.make_async_remote_copy(
            src_ref=ret_ref.at[slot, peer],
            dst_ref=got_ref.at[16 * slot + me],
            send_sem=back_send.at[slot, peer],
            recv_sem=back_recv.at[slot, me],
            device_id={"mem": peer},
            device_id_type=MESH,
        )

    def attend(slot, carry):
        def arrived(step, carry):
            peer = lax.rem(me + step, PEERS)
            pltpu.make_async_remote_copy(
                src_ref=send_ref.at[16 * slot + peer],
                dst_ref=recv_ref.at[slot, peer],
                send_sem=go_send.at[slot, peer],
                recv_sem=go_recv.at[slot, peer],
                device_id={"mem": peer},
                device_id_type=MESH,
            ).wait_recv()
            return carry

        lax.fori_loop(1, PEERS, arrived, 0)

        def prepare(group, carry):
            values = recv_ref[slot, pl.ds(4 * group, 4)].astype(F32).reshape(8, 32, 128)
            centred = values - jnp.mean(values, axis=1, keepdims=True)
            spread = jnp.mean(centred * centred, axis=1, keepdims=True)
            normed = centred * lax.rsqrt(spread + 1e-05) * gcol_ref[...][None]
            out = dot(proj_ref[...], normed.astype(BF).reshape(256, 128))
            out = out.astype(BF).astype(F32)
            q_ref[group] = (out[0:256] * scale).reshape(32, 8, 128)
            k_ref[group] = out[256:512].reshape(32, 8, 128)
            v_ref[group] = out[512:768].reshape(32, 8, 128)
            return carry

        lax.fori_loop(0, 4, prepare, 0, unroll=4)

        def head(h, carry):
            queries = [[q_ref[mb, 8 * h + d] for mb in range(4)] for d in range(8)]

            def score(group, peak):
                peak = list(peak)
                for n in range(8):
                    total = [None] * 4
                    for d in range(8):
                        key = jnp.broadcast_to(k_ref[group, 8 * h + d, n : n + 1, :], (8, 128))
                        for mb in range(4):
                            term = queries[d][mb] * key
                            total[mb] = term if d == 0 else total[mb] + term
                    for mb in range(4):
                        s_ref[8 * group + n, mb] = total[mb]
                        peak[mb] = jnp.maximum(peak[mb], total[mb])
                return tuple(peak)

            low = jnp.full((8, 128), -jnp.inf, F32)
            peak = lax.fori_loop(0, 4, score, (low,) * 4)

            def mix(group, state):
                weight, mixed = list(state[0]), [list(m) for m in state[1]]
                for n in range(8):
                    probs = [jnp.exp2(s_ref[8 * group + n, mb] - peak[mb]) for mb in range(4)]
                    for mb in range(4):
                        weight[mb] = weight[mb] + probs[mb]
                    for d in range(8):
                        value = jnp.broadcast_to(v_ref[group, 8 * h + d, n : n + 1, :], (8, 128))
                        for mb in range(4):
                            mixed[d][mb] = mixed[d][mb] + probs[mb] * value
                return tuple(weight), tuple(tuple(m) for m in mixed)

            zero = jnp.zeros((8, 128), F32)
            weight, mixed = lax.fori_loop(0, 4, mix, ((zero,) * 4, ((zero,) * 4,) * 8))
            for mb in range(4):
                inverse = 1.0 / weight[mb]
                for d in range(8):
                    mix_ref[mb, 8 * h + d] = mixed[d][mb] * inverse
            return carry

        lax.fori_loop(0, HEADS, head, 0)

        for step in range(4):
            group = lax.rem(step + me // 4, 4)
            mixed = mix_ref[group].reshape(256, 128).astype(BF)
            state = recv_ref[slot, pl.ds(4 * group, 4)].astype(F32).reshape(256, 128)
            final = dot(back_ref[...], mixed) + state
            ret_ref[slot, pl.ds(4 * group, 4)] = final.astype(BF).reshape(4, 2, 32, 128)
            if step == 0:
                got_ref[16 * slot + me] = ret_ref[slot, me]
            for row in range(1 if step == 0 else 0, 4):
                back(slot, 4 * group + lax.rem(me + row, 4)).start()
        return carry

    lax.fori_loop(0, 2, attend, 0)

    def returned(slot, carry):
        def one(step, carry):
            peer = lax.rem(me + step, PEERS)
            pltpu.make_async_remote_copy(
                src_ref=ret_ref.at[slot, peer],
                dst_ref=got_ref.at[16 * slot + peer],
                send_sem=back_send.at[slot, peer],
                recv_sem=back_recv.at[slot, peer],
                device_id={"mem": peer},
                device_id_type=MESH,
            ).wait_recv()
            return carry

        lax.fori_loop(1, PEERS, one, 0)

        def place(lat, carry):
            for m in range(2):
                z_ref[m, pl.ds(16 * slot + lat, 32, stride=32), :] = got_ref[
                    16 * slot + lat, m
                ].astype(F32)
            return carry

        lax.fori_loop(0, 16, place, 0, unroll=16)
        return carry

    lax.fori_loop(0, 2, returned, 0)
    for m in range(2):
        out_ref[m] = z_ref[m].astype(BF).reshape(32, 32, 128)

    def sent(step, carry):
        peer = lax.rem(me + step, PEERS)
        for slot in range(2):
            go(slot, peer).wait_send()
            back(slot, peer).wait_send()
        return carry

    lax.fori_loop(1, PEERS, sent, 0)


def on_device(members, conv_one, conv_two, conv_three, norm_gain, w_query, w_key, w_value, w_out):
    taps = [jnp.transpose(w, (2, 3, 0, 1)) for w in (conv_one, conv_two, conv_three)]
    vmem = pl.BlockSpec(memory_space=pltpu.VMEM)
    return pl.pallas_call(
        kernel,
        out_shape=jax.ShapeDtypeStruct(members.shape, BF),
        in_specs=[pl.BlockSpec(memory_space=pltpu.HBM)] * 9,
        out_specs=vmem,
        scratch_shapes=[
            pltpu.VMEM((2, 32, 32, 128), BF),
            pltpu.VMEM((5, 5, 32, 32), BF),
            pltpu.VMEM((5, 5, 32, 32), BF),
            pltpu.VMEM((5, 5, 32, 32), BF),
            pltpu.VMEM((1, 32), F32),
            pltpu.VMEM((32, 32), BF),
            pltpu.VMEM((32, 32), BF),
            pltpu.VMEM((32, 32), BF),
            pltpu.VMEM((32, 32), BF),
            pltpu.VMEM((2, 1024, 128), F32),
            pltpu.VMEM((1152, 384), BF),
            pltpu.VMEM((1152, 384), BF),
            pltpu.VMEM((1152, 384), BF),
            pltpu.VMEM((3, 640, 256), BF),
            pltpu.VMEM((768, 256), BF),
            pltpu.VMEM((256, 256), BF),
            pltpu.VMEM((32, 128), F32),
            pltpu.VMEM((2, 16, 1024), BF),
            pltpu.VMEM((2, 16, 1024), BF),
            pltpu.VMEM((32, 2, 32, 128), BF),
            pltpu.VMEM((2, 16, 2, 32, 128), BF),
            pltpu.VMEM((4, 32, 8, 128), F32),
            pltpu.VMEM((4, 32, 8, 128), F32),
            pltpu.VMEM((4, 32, 8, 128), F32),
            pltpu.VMEM((32, 4, 8, 128), F32),
            pltpu.VMEM((4, 32, 8, 128), F32),
            pltpu.VMEM((2, 16, 2, 32, 128), BF),
            pltpu.VMEM((32, 2, 32, 128), BF),
            pltpu.SemaphoreType.DMA((2,)),
            pltpu.SemaphoreType.DMA((2,)),
            pltpu.SemaphoreType.DMA((2, 16)),
            pltpu.SemaphoreType.DMA((2, 16)),
            pltpu.SemaphoreType.DMA((2, 16)),
            pltpu.SemaphoreType.DMA((2, 16)),
            pltpu.SemaphoreType.DMA((9,)),
        ],
        compiler_params=pltpu.CompilerParams(
            collective_id=0, has_side_effects=True, vmem_limit_bytes=56 * 1024 * 1024
        ),
    )(members, *taps, norm_gain.reshape(1, 32), w_query, w_key, w_value, w_out)


def solution(mesh):
    in_specs = (P("mem", None, None, "lon"), P(), P(), P(), P(), P(), P(), P(), P())
    out_specs = P("mem", None, None, "lon")
    return jax.shard_map(
        on_device, mesh=mesh, in_specs=in_specs, out_specs=out_specs, check_vma=False
    )
```

```python
import math

import jax
import jax.numpy as jnp
from jax import lax
from jax.experimental import pallas as pl
from jax.experimental.pallas import tpu as pltpu
from jax.sharding import PartitionSpec as P

MESH = pl.DeviceIdType.MESH
HEADS = 4
BF = jnp.bfloat16
F32 = jnp.float32
PEERS = 16


def iota(shape, dim):
    return lax.broadcasted_iota(jnp.int32, shape, dim)


def ones_where(mask):
    return jnp.where(mask, 1.0, 0.0).astype(BF)


def dot(a, b, contract=((1,), (0,))):
    return lax.dot_general(a, b, (contract, ((), ())), preferred_element_type=F32)


def device(**where):
    return {name: index for name, index in where.items()}


def kernel(
    x_hbm,
    w1_hbm,
    w2_hbm,
    w3_hbm,
    gain_hbm,
    wq_hbm,
    wk_hbm,
    wv_hbm,
    wo_hbm,
    out_ref,
    x_ref,
    w1_ref,
    w2_ref,
    w3_ref,
    gain_ref,
    wq_ref,
    wk_ref,
    wv_ref,
    wo_ref,
    z_ref,
    xa_ref,
    xb_ref,
    xc_ref,
    band_ref,
    proj_ref,
    back_ref,
    gcol_ref,
    hs_ref,
    hr_ref,
    send_ref,
    recv_ref,
    q_ref,
    k_ref,
    v_ref,
    s_ref,
    mix_ref,
    ret_ref,
    got_ref,
    halo_send,
    halo_recv,
    go_send,
    go_recv,
    back_send,
    back_recv,
    load_sem,
):
    loads = [
        pltpu.make_async_copy(source, target, load_sem.at[index])
        for index, (source, target) in enumerate(
            (
                (x_hbm, x_ref),
                (w1_hbm, w1_ref),
                (w2_hbm, w2_ref),
                (w3_hbm, w3_ref),
                (gain_hbm, gain_ref),
                (wq_hbm, wq_ref),
                (wk_hbm, wk_ref),
                (wv_hbm, wv_ref),
                (wo_hbm, wo_ref),
            )
        )
    ]
    for load in loads:
        load.start()
    me = lax.axis_index("mem")
    col = lax.axis_index("lon")
    right, left = lax.rem(col + 1, PEERS), lax.rem(col + PEERS - 1, PEERS)

    barrier = pltpu.get_barrier_semaphore()

    def greet(step, carry):
        pl.semaphore_signal(
            barrier, inc=1, device_id={"mem": lax.rem(me + step, PEERS)}, device_id_type=MESH
        )
        return carry

    for side in (left, right):
        pl.semaphore_signal(barrier, inc=1, device_id={"lon": side}, device_id_type=MESH)
    lax.fori_loop(1, PEERS, greet, 0)

    for buf in (xa_ref, xb_ref, xc_ref):
        buf[0:64, :] = jnp.zeros((64, 384), BF)
        buf[1088:1152, :] = jnp.zeros((64, 384), BF)
    loads[0].wait()
    for m in range(2):
        z_ref[m] = x_ref[m].astype(F32).reshape(1024, 128)
        for lat in range(32):
            rows = z_ref[m, pl.ds(lat, 32, stride=32), :]
            xa_ref[64 + 32 * lat : 96 + 32 * lat, 128 * m : 128 * m + 128] = rows.astype(BF)

    r, lane = iota((32, 256), 0), iota((32, 256), 1)
    want = jnp.where(r < 16, 0, 120) + (r & 7) + jnp.where((r & 8) != 0, 128, 0)
    edges = dot(ones_where(lane == want), xa_ref[64:1088, 0:256], ((1,), (1,)))
    edges = edges.astype(BF)
    hs_ref[0] = edges[0:16]
    hs_ref[1] = edges[16:32]

    pl.semaphore_wait(barrier, PEERS + 1)

    def halo(side, target):
        return pltpu.make_async_remote_copy(
            src_ref=hs_ref.at[side],
            dst_ref=hr_ref.at[side],
            send_sem=halo_send.at[side],
            recv_sem=halo_recv.at[side],
            device_id={"lon": target},
            device_id_type=MESH,
        )

    to_left, to_right = halo(0, left), halo(1, right)
    to_left.start()
    to_right.start()

    for load in loads[1:]:
        load.wait()

    for layer, w_ref in enumerate((w1_ref, w2_ref, w3_ref)):
        for dx in range(5):
            pieces = [w_ref[dy, dx].astype(F32) for dy in range(5)]
            base = jnp.concatenate(pieces + [jnp.zeros((32, 96), F32)], axis=1)
            for up in range(4):
                rolled = base if up == 0 else pltpu.roll(base, 32 * up, 1)
                at = dx * 128 + up * 32
                band_ref[layer, at : at + 32, :] = rolled.astype(BF)

    def convolve(source, layer, block, tiles):
        rows = pl.ds(pl.multiple_of(block * 128, 128), 256)
        window = source[rows, 128 * tiles[0] : 128 * tiles[-1] + 128]
        total = [None] * len(tiles)
        for dx in range(5):
            y = dot(band_ref[layer, dx * 128 : dx * 128 + 128, :], window)
            for t in range(len(tiles)):
                part = y[:, 128 * t : 128 * t + 128]
                if dx != 2:
                    part = pltpu.roll(part, (2 - dx) % 128, 1)
                total[t] = part if total[t] is None else total[t] + part
        return total

    def silu_layer(source, target, layer, blocks, tiles):
        for block in blocks:
            total = convolve(source, layer, block, tiles)
            for t, value in zip(tiles, total):
                value = 0.5 * value
                value = value * jnp.tanh(value) + value
                at = 64 + 128 * block
                target[at : at + 128, 128 * t : 128 * t + 128] = value.astype(BF)

    def go(slot, peer):
        return pltpu.make_async_remote_copy(
            src_ref=send_ref.at[16 * slot + peer],
            dst_ref=recv_ref.at[slot, me],
            send_sem=go_send.at[slot, peer],
            recv_sem=go_recv.at[slot, me],
            device_id={"mem": peer},
            device_id_type=MESH,
        )

    quarter = me // 4
    half, odd = quarter // 2, lax.rem(quarter, 2)
    order = (2 * (1 - half) + odd, 3 - 2 * half - odd, 2 * half + 1 - odd, quarter)

    def peers_of(step):
        first = 1 if step == 3 else 0
        return [4 * order[step] + lax.rem(me + row, 4) for row in range(first, 4)]

    def residual(block, t, total):
        at = pl.ds(pl.multiple_of(64 + block * 128, 64), 128)
        value = total + xa_ref[at, 128 * t : 128 * t + 128].astype(F32)
        return value.astype(BF)

    silu_layer(xa_ref, xb_ref, 0, range(8), (0, 1))
    silu_layer(xb_ref, xc_ref, 1, range(8), (0, 1))
    for block in range(8):
        total = convolve(xc_ref, 2, block, (0, 1))
        for m in range(2):
            state = residual(block, m, total[m])
            for row in range(4):
                send_ref[4 * block + row, m] = state[32 * row : 32 * row + 32]

    to_left.wait()
    to_right.wait()

    r, lane = iota((256, 128), 0), iota((256, 128), 1)
    lon, base = r & 127, (r >> 7) * 64
    inner = jnp.where(lon < 16, base + 16 + lon, jnp.where(lon >= 112, base + lon - 80, -1))
    r2, lane2 = iota((32, 128), 0), iota((32, 128), 1)
    outer = jnp.where(r2 < 16, 48, 8) + (r2 & 7) + jnp.where((r2 & 8) != 0, 64, 0)
    strip = dot(xa_ref[64:1088, 0:256], ones_where(lane == inner))
    ring = hr_ref[...].reshape(32, 1024)
    strip = strip + dot(ring, ones_where(lane2 == outer), ((0,), (0,)))
    xa_ref[64:1088, 256:384] = strip.astype(BF)

    def edges_and_go(slot):
        for step in range(4):
            block = 4 * slot + order[step]
            strip = residual(block, 2, convolve(xc_ref, 2, block, (2,))[0]).astype(F32)
            lane = iota((128, 128), 1)
            for m in range(2):
                low = pltpu.roll(strip, 112 - 64 * m, 1)
                high = pltpu.roll(strip, (80 - 64 * m) % 128, 1)
                edge = jnp.where(lane < 8, low, high).reshape(4, 32, 128)
                inside = (iota((4, 32, 128), 2) >= 8) & (iota((4, 32, 128), 2) < 120)
                rows = pl.ds(4 * block, 4)
                whole = jnp.where(inside, send_ref[rows, m].astype(F32), edge)
                send_ref[rows, m] = whole.astype(BF)
            if step == 3:
                recv_ref[slot, me] = send_ref[16 * slot + me]
            for peer in peers_of(step):
                go(slot, peer).start()

    silu_layer(xa_ref, xb_ref, 0, range(0, 6), (2,))
    silu_layer(xb_ref, xc_ref, 1, range(0, 5), (2,))
    edges_and_go(0)
    silu_layer(xa_ref, xb_ref, 0, range(6, 8), (2,))
    silu_layer(xb_ref, xc_ref, 1, range(5, 8), (2,))
    edges_and_go(1)

    r, c = iota((256, 32), 0), iota((256, 32), 1)
    spread = ones_where((r >> 3) == c)
    spread_out = ones_where((r & 31) == c)
    c, lane = iota((32, 256), 0), iota((32, 256), 1)
    tile = ones_where((lane & 31) == c)
    tile_out = ones_where((lane >> 3) == c)
    r, lane = iota((256, 256), 0), iota((256, 256), 1)
    own = (r & 7) == (lane >> 5)
    own_out = (r >> 5) == (lane & 7)
    for index, w_ref in enumerate((wq_ref, wk_ref, wv_ref)):
        tall = dot(spread, w_ref[...], ((1,), (1,))).astype(BF)
        full = jnp.where(own, dot(tall, tile), 0.0)
        proj_ref[256 * index : 256 * index + 256, :] = full.astype(BF)
    tall = dot(spread_out, wo_ref[...], ((1,), (1,))).astype(BF)
    back_ref[...] = jnp.where(own_out, dot(tall, tile_out), 0.0).astype(BF)
    eye = iota((32, 32), 0) == iota((32, 32), 1)
    gains = jnp.broadcast_to(gain_ref[...], (32, 32))
    gcol = jnp.sum(jnp.where(eye, gains, 0.0), axis=1, keepdims=True)
    gcol_ref[...] = jnp.broadcast_to(gcol, (32, 128))

    scale = math.log2(math.e) / math.sqrt(32 // HEADS)

    def back(slot, peer):
        return pltpu.make_async_remote_copy(
            src_ref=ret_ref.at[slot, peer],
            dst_ref=got_ref.at[16 * slot + me],
            send_sem=back_send.at[slot, peer],
            recv_sem=back_recv.at[slot, me],
            device_id={"mem": peer},
            device_id_type=MESH,
        )

    def attend(slot, carry):
        for step in (3, 2, 0, 1):
            group = order[step]
            for peer in peers_of(step):
                pltpu.make_async_remote_copy(
                    src_ref=send_ref.at[16 * slot + peer],
                    dst_ref=recv_ref.at[slot, peer],
                    send_sem=go_send.at[slot, peer],
                    recv_sem=go_recv.at[slot, peer],
                    device_id={"mem": peer},
                    device_id_type=MESH,
                ).wait_recv()
            values = recv_ref[slot, pl.ds(4 * group, 4)].astype(F32).reshape(8, 32, 128)
            centred = values - jnp.mean(values, axis=1, keepdims=True)
            spread = jnp.mean(centred * centred, axis=1, keepdims=True)
            normed = centred * lax.rsqrt(spread + 1e-05) * gcol_ref[...][None]
            out = dot(proj_ref[...], normed.astype(BF).reshape(256, 128))
            out = out.astype(BF).astype(F32)
            q_ref[group] = (out[0:256] * scale).reshape(32, 8, 128)
            k_ref[group] = out[256:512].reshape(32, 8, 128)
            v_ref[group] = out[512:768].reshape(32, 8, 128)

        for pair in range(2):
            groups = (order[2 * pair], order[2 * pair + 1])

            def head(h, carry):
                queries = [[q_ref[group, 8 * h + d] for group in groups] for d in range(8)]

                def score(group, peak):
                    peak = list(peak)
                    for n in range(8):
                        total = [None] * 2
                        for d in range(8):
                            key = jnp.broadcast_to(k_ref[group, 8 * h + d, n : n + 1, :], (8, 128))
                            for i in range(2):
                                term = queries[d][i] * key
                                total[i] = term if d == 0 else total[i] + term
                        for i in range(2):
                            s_ref[8 * group + n, i] = total[i]
                            peak[i] = jnp.maximum(peak[i], total[i])
                    return tuple(peak)

                low = jnp.full((8, 128), -jnp.inf, F32)
                peak = lax.fori_loop(0, 4, score, (low,) * 2)

                def mix(group, state):
                    weight, mixed = list(state[0]), [list(m) for m in state[1]]
                    for n in range(8):
                        probs = [jnp.exp2(s_ref[8 * group + n, i] - peak[i]) for i in range(2)]
                        for i in range(2):
                            weight[i] = weight[i] + probs[i]
                        for d in range(8):
                            value = jnp.broadcast_to(
                                v_ref[group, 8 * h + d, n : n + 1, :], (8, 128)
                            )
                            for i in range(2):
                                mixed[d][i] = mixed[d][i] + probs[i] * value
                    return tuple(weight), tuple(tuple(m) for m in mixed)

                zero = jnp.zeros((8, 128), F32)
                weight, mixed = lax.fori_loop(0, 4, mix, ((zero,) * 2, ((zero,) * 2,) * 8))
                for i in range(2):
                    inverse = 1.0 / weight[i]
                    for d in range(8):
                        mix_ref[i, 8 * h + d] = mixed[d][i] * inverse
                return carry

            lax.fori_loop(0, HEADS, head, 0)

            for i in range(2):
                step = 2 * pair + i
                group = order[step]
                mixed = mix_ref[i].reshape(256, 128).astype(BF)
                state = recv_ref[slot, pl.ds(4 * group, 4)].astype(F32).reshape(256, 128)
                final = dot(back_ref[...], mixed) + state
                ret_ref[slot, pl.ds(4 * group, 4)] = final.astype(BF).reshape(4, 2, 32, 128)
                if step == 3:
                    got_ref[16 * slot + me] = ret_ref[slot, me]
                for peer in peers_of(step):
                    back(slot, peer).start()
        return carry

    lax.fori_loop(0, 2, attend, 0)

    def returned(slot, carry):
        for step in range(4):
            for peer in peers_of(step):
                pltpu.make_async_remote_copy(
                    src_ref=ret_ref.at[slot, peer],
                    dst_ref=got_ref.at[16 * slot + peer],
                    send_sem=back_send.at[slot, peer],
                    recv_sem=back_recv.at[slot, peer],
                    device_id={"mem": peer},
                    device_id_type=MESH,
                ).wait_recv()
            for row in range(4):
                lat = 16 * slot + 4 * order[step] + row
                for m in range(2):
                    z_ref[m, pl.ds(lat, 32, stride=32), :] = got_ref[lat, m].astype(F32)
        return carry

    lax.fori_loop(0, 2, returned, 0)
    for m in range(2):
        out_ref[m] = z_ref[m].astype(BF).reshape(32, 32, 128)

    def sent(step, carry):
        peer = lax.rem(me + step, PEERS)
        for slot in range(2):
            go(slot, peer).wait_send()
            back(slot, peer).wait_send()
        return carry

    lax.fori_loop(1, PEERS, sent, 0)


def on_device(members, conv_one, conv_two, conv_three, norm_gain, w_query, w_key, w_value, w_out):
    taps = [jnp.transpose(w, (2, 3, 0, 1)) for w in (conv_one, conv_two, conv_three)]
    vmem = pl.BlockSpec(memory_space=pltpu.VMEM)
    operands = (members, *taps, norm_gain.reshape(1, 32), w_query, w_key, w_value, w_out)
    return pl.pallas_call(
        kernel,
        out_shape=jax.ShapeDtypeStruct(members.shape, BF),
        in_specs=[pl.BlockSpec(memory_space=pltpu.HBM)] * 9,
        out_specs=vmem,
        scratch_shapes=[
            pltpu.VMEM((2, 32, 32, 128), BF),
            pltpu.VMEM((5, 5, 32, 32), BF),
            pltpu.VMEM((5, 5, 32, 32), BF),
            pltpu.VMEM((5, 5, 32, 32), BF),
            pltpu.VMEM((1, 32), F32),
            pltpu.VMEM((32, 32), BF),
            pltpu.VMEM((32, 32), BF),
            pltpu.VMEM((32, 32), BF),
            pltpu.VMEM((32, 32), BF),
            pltpu.VMEM((2, 1024, 128), F32),
            pltpu.VMEM((1152, 384), BF),
            pltpu.VMEM((1152, 384), BF),
            pltpu.VMEM((1152, 384), BF),
            pltpu.VMEM((3, 640, 256), BF),
            pltpu.VMEM((768, 256), BF),
            pltpu.VMEM((256, 256), BF),
            pltpu.VMEM((32, 128), F32),
            pltpu.VMEM((2, 16, 1024), BF),
            pltpu.VMEM((2, 16, 1024), BF),
            pltpu.VMEM((32, 2, 32, 128), BF),
            pltpu.VMEM((2, 16, 2, 32, 128), BF),
            pltpu.VMEM((4, 32, 8, 128), F32),
            pltpu.VMEM((4, 32, 8, 128), F32),
            pltpu.VMEM((4, 32, 8, 128), F32),
            pltpu.VMEM((32, 2, 8, 128), F32),
            pltpu.VMEM((2, 32, 8, 128), F32),
            pltpu.VMEM((2, 16, 2, 32, 128), BF),
            pltpu.VMEM((32, 2, 32, 128), BF),
            pltpu.SemaphoreType.DMA((2,)),
            pltpu.SemaphoreType.DMA((2,)),
            pltpu.SemaphoreType.DMA((2, 16)),
            pltpu.SemaphoreType.DMA((2, 16)),
            pltpu.SemaphoreType.DMA((2, 16)),
            pltpu.SemaphoreType.DMA((2, 16)),
            pltpu.SemaphoreType.DMA((9,)),
        ],
        compiler_params=pltpu.CompilerParams(
            collective_id=0, has_side_effects=True, vmem_limit_bytes=40 * 1024 * 1024
        ),
    )(*[pltpu.with_memory_space_constraint(value, pltpu.HBM) for value in operands])


def solution(mesh):
    in_specs = (P("mem", None, None, "lon"), P(), P(), P(), P(), P(), P(), P(), P())
    out_specs = P("mem", None, None, "lon")
    return jax.shard_map(
        on_device, mesh=mesh, in_specs=in_specs, out_specs=out_specs, check_vma=False
    )
```

```python
import math

import jax
import jax.numpy as jnp
from jax import lax
from jax.experimental import pallas as pl
from jax.experimental.pallas import tpu as pltpu
from jax.sharding import PartitionSpec as P

MESH = pl.DeviceIdType.MESH
HEADS = 4
BF = jnp.bfloat16
F32 = jnp.float32
PEERS = 16


def iota(shape, dim):
    return lax.broadcasted_iota(jnp.int32, shape, dim)


def ones_where(mask):
    return jnp.where(mask, 1.0, 0.0).astype(BF)


def dot(a, b, contract=((1,), (0,))):
    return lax.dot_general(a, b, (contract, ((), ())), preferred_element_type=F32)


def device(**where):
    return {name: index for name, index in where.items()}


def kernel(
    x_hbm,
    w1_hbm,
    w2_hbm,
    w3_hbm,
    gain_hbm,
    wq_hbm,
    wk_hbm,
    wv_hbm,
    wo_hbm,
    out_ref,
    x_ref,
    w1_ref,
    w2_ref,
    w3_ref,
    gain_ref,
    wq_ref,
    wk_ref,
    wv_ref,
    wo_ref,
    z_ref,
    xa_ref,
    xb_ref,
    xc_ref,
    band_ref,
    proj_ref,
    back_ref,
    gcol_ref,
    hs_ref,
    hr_ref,
    send_ref,
    recv_ref,
    q_ref,
    k_ref,
    v_ref,
    s_ref,
    peak_ref,
    packed_ref,
    es_ref,
    er_ref,
    edges_ref,
    state_ref,
    mix_ref,
    ret_ref,
    got_ref,
    halo_send,
    halo_recv,
    go_send,
    go_recv,
    back_send,
    back_recv,
    edge_send,
    edge_recv,
    load_sem,
):
    loads = [
        pltpu.make_async_copy(source, target, load_sem.at[index])
        for index, (source, target) in enumerate(
            (
                (x_hbm, x_ref),
                (w1_hbm, w1_ref),
                (w2_hbm, w2_ref),
                (w3_hbm, w3_ref),
                (gain_hbm, gain_ref),
                (wq_hbm, wq_ref),
                (wk_hbm, wk_ref),
                (wv_hbm, wv_ref),
                (wo_hbm, wo_ref),
            )
        )
    ]
    for load in loads:
        load.start()
    me = lax.axis_index("mem")
    col = lax.axis_index("lon")
    right, left = lax.rem(col + 1, PEERS), lax.rem(col + PEERS - 1, PEERS)

    barrier = pltpu.get_barrier_semaphore()

    def greet(step, carry):
        pl.semaphore_signal(
            barrier, inc=1, device_id={"mem": lax.rem(me + step, PEERS)}, device_id_type=MESH
        )
        return carry

    for side in (left, right):
        pl.semaphore_signal(barrier, inc=1, device_id={"lon": side}, device_id_type=MESH)
    lax.fori_loop(1, PEERS, greet, 0)

    for buf in (xa_ref, xb_ref, xc_ref):
        buf[0:64, :] = jnp.zeros((64, 384), BF)
        buf[1088:1152, :] = jnp.zeros((64, 384), BF)
    loads[0].wait()
    for m in range(2):
        z_ref[m] = x_ref[m].astype(F32).reshape(1024, 128)
        for lat in range(32):
            rows = z_ref[m, pl.ds(lat, 32, stride=32), :]
            xa_ref[64 + 32 * lat : 96 + 32 * lat, 128 * m : 128 * m + 128] = rows.astype(BF)

    r, lane = iota((32, 256), 0), iota((32, 256), 1)
    want = jnp.where(r < 16, 0, 120) + (r & 7) + jnp.where((r & 8) != 0, 128, 0)
    edges = dot(ones_where(lane == want), xa_ref[64:1088, 0:256], ((1,), (1,)))
    edges = edges.astype(BF)
    hs_ref[0] = edges[0:16]
    hs_ref[1] = edges[16:32]

    pl.semaphore_wait(barrier, PEERS + 1)

    def halo(side, target):
        return pltpu.make_async_remote_copy(
            src_ref=hs_ref.at[side],
            dst_ref=hr_ref.at[side],
            send_sem=halo_send.at[side],
            recv_sem=halo_recv.at[side],
            device_id={"lon": target},
            device_id_type=MESH,
        )

    to_left, to_right = halo(0, left), halo(1, right)
    to_left.start()
    to_right.start()

    for load in loads[1:]:
        load.wait()

    for layer, w_ref in enumerate((w1_ref, w2_ref, w3_ref)):
        for dx in range(5):
            pieces = [w_ref[dy, dx].astype(F32) for dy in range(5)]
            base = jnp.concatenate(pieces + [jnp.zeros((32, 96), F32)], axis=1)
            for up in range(4):
                rolled = base if up == 0 else pltpu.roll(base, 32 * up, 1)
                at = dx * 128 + up * 32
                band_ref[layer, at : at + 32, :] = rolled.astype(BF)

    def convolve(source, layer, block, tiles):
        rows = pl.ds(pl.multiple_of(block * 128, 128), 256)
        window = source[rows, 128 * tiles[0] : 128 * tiles[-1] + 128]
        total = [None] * len(tiles)
        for dx in range(5):
            y = dot(band_ref[layer, dx * 128 : dx * 128 + 128, :], window)
            for t in range(len(tiles)):
                part = y[:, 128 * t : 128 * t + 128]
                if dx != 2:
                    part = pltpu.roll(part, (2 - dx) % 128, 1)
                total[t] = part if total[t] is None else total[t] + part
        return total

    def silu_layer(source, target, layer, blocks, tiles):
        for block in blocks:
            total = convolve(source, layer, block, tiles)
            for t, value in zip(tiles, total):
                value = 0.5 * value
                value = value * jnp.tanh(value) + value
                at = 64 + 128 * block
                target[at : at + 128, 128 * t : 128 * t + 128] = value.astype(BF)

    def go(slot, peer):
        return pltpu.make_async_remote_copy(
            src_ref=send_ref.at[16 * slot + peer],
            dst_ref=recv_ref.at[slot, me],
            send_sem=go_send.at[slot, peer],
            recv_sem=go_recv.at[slot, me],
            device_id={"mem": peer},
            device_id_type=MESH,
        )

    quarter = me // 4
    half, odd = quarter // 2, lax.rem(quarter, 2)
    order = (2 * (1 - half) + odd, 3 - 2 * half - odd, 2 * half + 1 - odd, quarter)

    def peers_of(step):
        first = 1 if step == 3 else 0
        return [4 * order[step] + lax.rem(me + row, 4) for row in range(first, 4)]

    def residual(block, t, total):
        at = pl.ds(pl.multiple_of(64 + block * 128, 64), 128)
        value = total + xa_ref[at, 128 * t : 128 * t + 128].astype(F32)
        return value.astype(BF)

    def main_and_go(slot):
        for step in range(4):
            block = 4 * slot + order[step]
            total = convolve(xc_ref, 2, block, (0, 1))
            for m in range(2):
                state = residual(block, m, total[m])
                send_ref[pl.ds(4 * block, 4), m] = state.reshape(4, 32, 128)
            if step == 3:
                recv_ref[slot, me] = send_ref[16 * slot + me]
            for peer in peers_of(step):
                go(slot, peer).start()

    silu_layer(xa_ref, xb_ref, 0, range(0, 6), (0, 1))
    silu_layer(xb_ref, xc_ref, 1, range(0, 5), (0, 1))
    main_and_go(0)
    silu_layer(xa_ref, xb_ref, 0, range(6, 8), (0, 1))
    silu_layer(xb_ref, xc_ref, 1, range(5, 8), (0, 1))
    main_and_go(1)

    to_left.wait()
    to_right.wait()

    r, lane = iota((256, 128), 0), iota((256, 128), 1)
    lon, base = r & 127, (r >> 7) * 64
    inner = jnp.where(lon < 16, base + 16 + lon, jnp.where(lon >= 112, base + lon - 80, -1))
    r2, lane2 = iota((32, 128), 0), iota((32, 128), 1)
    outer = jnp.where(r2 < 16, 48, 8) + (r2 & 7) + jnp.where((r2 & 8) != 0, 64, 0)
    strip = dot(xa_ref[64:1088, 0:256], ones_where(lane == inner))
    ring = hr_ref[...].reshape(32, 1024)
    strip = strip + dot(ring, ones_where(lane2 == outer), ((0,), (0,)))
    xa_ref[64:1088, 256:384] = strip.astype(BF)

    silu_layer(xa_ref, xb_ref, 0, range(8), (2,))
    silu_layer(xb_ref, xc_ref, 1, range(8), (2,))

    r, lane = iota((512, 128), 0), iota((512, 128), 1)
    inner, which = r & 127, lane & 31
    source = (which >> 4) * 64 + jnp.where((which & 8) != 0, 16, 40) + (which & 7)
    pack = ones_where(((r >> 7) == (lane >> 5)) & (inner == source))
    for block in range(8):
        strip = residual(block, 2, convolve(xc_ref, 2, block, (2,))[0]).astype(F32)
        strip = strip.reshape(4, 4, 8, 128)
        wide = jnp.concatenate([strip[:, o].reshape(32, 128) for o in range(4)], axis=1)
        packed_ref[4 * block : 4 * block + 4] = dot(wide.astype(BF), pack).reshape(4, 8, 128)
    for peer in range(PEERS):
        both = jnp.concatenate([packed_ref[peer], packed_ref[16 + peer]], axis=0)
        es_ref[peer] = both.astype(BF)

    def edge(peer):
        return pltpu.make_async_remote_copy(
            src_ref=es_ref.at[peer],
            dst_ref=er_ref.at[me],
            send_sem=edge_send.at[peer],
            recv_sem=edge_recv.at[me],
            device_id={"mem": peer},
            device_id_type=MESH,
        )

    er_ref[me] = es_ref[me]
    for step in range(4):
        for peer in peers_of(step):
            edge(peer).start()

    r, c = iota((256, 32), 0), iota((256, 32), 1)
    spread = ones_where((r >> 3) == c)
    spread_out = ones_where((r & 31) == c)
    c, lane = iota((32, 256), 0), iota((32, 256), 1)
    tile = ones_where((lane & 31) == c)
    tile_out = ones_where((lane >> 3) == c)
    r, lane = iota((256, 256), 0), iota((256, 256), 1)
    own = (r & 7) == (lane >> 5)
    own_out = (r >> 5) == (lane & 7)
    for index, w_ref in enumerate((wq_ref, wk_ref, wv_ref)):
        tall = dot(spread, w_ref[...], ((1,), (1,))).astype(BF)
        full = jnp.where(own, dot(tall, tile), 0.0)
        proj_ref[256 * index : 256 * index + 256, :] = full.astype(BF)
    tall = dot(spread_out, wo_ref[...], ((1,), (1,))).astype(BF)
    back_ref[...] = jnp.where(own_out, dot(tall, tile_out), 0.0).astype(BF)
    eye = iota((32, 32), 0) == iota((32, 32), 1)
    gains = jnp.broadcast_to(gain_ref[...], (32, 32))
    gcol = jnp.sum(jnp.where(eye, gains, 0.0), axis=1, keepdims=True)
    gcol_ref[...] = jnp.broadcast_to(gcol, (32, 128))

    scale = math.log2(math.e) / math.sqrt(32 // HEADS)

    def back(slot, peer):
        return pltpu.make_async_remote_copy(
            src_ref=ret_ref.at[slot, peer],
            dst_ref=got_ref.at[16 * slot + me],
            send_sem=back_send.at[slot, peer],
            recv_sem=back_recv.at[slot, me],
            device_id={"mem": peer},
            device_id_type=MESH,
        )

    def attend(slot, carry):
        for step in (3, 2, 0, 1):
            group = order[step]
            for peer in peers_of(step):
                pltpu.make_async_remote_copy(
                    src_ref=send_ref.at[16 * slot + peer],
                    dst_ref=recv_ref.at[slot, peer],
                    send_sem=go_send.at[slot, peer],
                    recv_sem=go_recv.at[slot, peer],
                    device_id={"mem": peer},
                    device_id_type=MESH,
                ).wait_recv()
            lane = iota((8, 128), 1)
            inside = (lane >= 8) & (lane < 120)
            rows = []
            for row in range(4):
                outer = edges_ref[4 * group + row, slot]
                for m in range(2):
                    main = recv_ref[slot, 4 * group + row, m].astype(F32)
                    for o in range(4):
                        turned = pltpu.roll(outer, (120 - 32 * o - 16 * m) % 128, 1)
                        rows.append(jnp.where(inside, main[8 * o : 8 * o + 8], turned))
            values = jnp.concatenate(rows, axis=0).reshape(8, 32, 128)
            state_ref[group] = values.reshape(256, 128)
            centred = values - jnp.mean(values, axis=1, keepdims=True)
            spread = jnp.mean(centred * centred, axis=1, keepdims=True)
            normed = centred * lax.rsqrt(spread + 1e-05) * gcol_ref[...][None]
            out = dot(proj_ref[...], normed.astype(BF).reshape(256, 128))
            out = out.astype(BF).astype(F32)
            q_ref[group] = (out[0:256] * scale).reshape(32, 8, 128)
            k_ref[group] = out[256:512].reshape(32, 8, 128)
            v_ref[group] = out[512:768].reshape(32, 8, 128)

        def head_scores(h, carry):
            queries = [[q_ref[order[i], 8 * h + d] for i in range(4)] for d in range(8)]

            def score(group, peak):
                peak = list(peak)
                for n in range(8):
                    total = [None] * 4
                    for d in range(8):
                        key = k_ref[group, 8 * h + d, pl.ds(n, 8, stride=0), :]
                        for i in range(4):
                            term = queries[d][i] * key
                            total[i] = term if d == 0 else total[i] + term
                    for i in range(4):
                        s_ref[h, 8 * group + n, i] = total[i]
                        peak[i] = jnp.maximum(peak[i], total[i])
                return tuple(peak)

            low = jnp.full((8, 128), -jnp.inf, F32)
            peak = lax.fori_loop(0, 4, score, (low,) * 4, unroll=2)
            for i in range(4):
                peak_ref[h, i] = peak[i]
            return carry

        lax.fori_loop(0, HEADS, head_scores, 0)

        for pair in range(2):

            def head_mix(h, carry):
                peak = [peak_ref[h, 2 * pair + i] for i in range(2)]

                def mix(group, state):
                    weight, mixed = list(state[0]), [list(m) for m in state[1]]
                    for n in range(8):
                        probs = [
                            jnp.exp2(s_ref[h, 8 * group + n, 2 * pair + i] - peak[i])
                            for i in range(2)
                        ]
                        for i in range(2):
                            weight[i] = weight[i] + probs[i]
                        for d in range(8):
                            value = v_ref[group, 8 * h + d, pl.ds(n, 8, stride=0), :]
                            for i in range(2):
                                mixed[d][i] = mixed[d][i] + probs[i] * value
                    return tuple(weight), tuple(tuple(m) for m in mixed)

                zero = jnp.zeros((8, 128), F32)
                start = ((zero,) * 2, ((zero,) * 2,) * 8)
                weight, mixed = lax.fori_loop(0, 4, mix, start, unroll=2)
                for i in range(2):
                    inverse = 1.0 / weight[i]
                    for d in range(8):
                        mix_ref[i, 8 * h + d] = mixed[d][i] * inverse
                return carry

            lax.fori_loop(0, HEADS, head_mix, 0)

            for i in range(2):
                step = 2 * pair + i
                group = order[step]
                mixed = mix_ref[i].reshape(256, 128).astype(BF)
                final = dot(back_ref[...], mixed) + state_ref[group]
                ret_ref[slot, pl.ds(4 * group, 4)] = final.astype(BF).reshape(4, 2, 32, 128)
                if step == 3:
                    got_ref[16 * slot + me] = ret_ref[slot, me]
                for peer in peers_of(step):
                    back(slot, peer).start()
        return carry

    for step in (3, 2, 0, 1):
        for peer in peers_of(step):
            pltpu.make_async_remote_copy(
                src_ref=es_ref.at[peer],
                dst_ref=er_ref.at[peer],
                send_sem=edge_send.at[peer],
                recv_sem=edge_recv.at[peer],
                device_id={"mem": peer},
                device_id_type=MESH,
            ).wait_recv()
    edges_ref[...] = er_ref[...].astype(F32).reshape(16, 2, 8, 128)

    lax.fori_loop(0, 2, attend, 0)

    def returned(slot, carry):
        for step in range(4):
            for peer in peers_of(step):
                pltpu.make_async_remote_copy(
                    src_ref=ret_ref.at[slot, peer],
                    dst_ref=got_ref.at[16 * slot + peer],
                    send_sem=back_send.at[slot, peer],
                    recv_sem=back_recv.at[slot, peer],
                    device_id={"mem": peer},
                    device_id_type=MESH,
                ).wait_recv()
            for row in range(4):
                lat = 16 * slot + 4 * order[step] + row
                for m in range(2):
                    z_ref[m, pl.ds(lat, 32, stride=32), :] = got_ref[lat, m].astype(F32)
        return carry

    lax.fori_loop(0, 2, returned, 0)
    for m in range(2):
        out_ref[m] = z_ref[m].astype(BF).reshape(32, 32, 128)

    def sent(step, carry):
        peer = lax.rem(me + step, PEERS)
        edge(peer).wait_send()
        for slot in range(2):
            go(slot, peer).wait_send()
            back(slot, peer).wait_send()
        return carry

    lax.fori_loop(1, PEERS, sent, 0)


def on_device(members, conv_one, conv_two, conv_three, norm_gain, w_query, w_key, w_value, w_out):
    taps = [jnp.transpose(w, (2, 3, 0, 1)) for w in (conv_one, conv_two, conv_three)]
    vmem = pl.BlockSpec(memory_space=pltpu.VMEM)
    operands = (members, *taps, norm_gain.reshape(1, 32), w_query, w_key, w_value, w_out)
    return pl.pallas_call(
        kernel,
        out_shape=jax.ShapeDtypeStruct(members.shape, BF),
        in_specs=[pl.BlockSpec(memory_space=pltpu.HBM)] * 9,
        out_specs=vmem,
        scratch_shapes=[
            pltpu.VMEM((2, 32, 32, 128), BF),
            pltpu.VMEM((5, 5, 32, 32), BF),
            pltpu.VMEM((5, 5, 32, 32), BF),
            pltpu.VMEM((5, 5, 32, 32), BF),
            pltpu.VMEM((1, 32), F32),
            pltpu.VMEM((32, 32), BF),
            pltpu.VMEM((32, 32), BF),
            pltpu.VMEM((32, 32), BF),
            pltpu.VMEM((32, 32), BF),
            pltpu.VMEM((2, 1024, 128), F32),
            pltpu.VMEM((1152, 384), BF),
            pltpu.VMEM((1152, 384), BF),
            pltpu.VMEM((1152, 384), BF),
            pltpu.VMEM((3, 640, 256), BF),
            pltpu.VMEM((768, 256), BF),
            pltpu.VMEM((256, 256), BF),
            pltpu.VMEM((32, 128), F32),
            pltpu.VMEM((2, 16, 1024), BF),
            pltpu.VMEM((2, 16, 1024), BF),
            pltpu.VMEM((32, 2, 32, 128), BF),
            pltpu.VMEM((2, 16, 2, 32, 128), BF),
            pltpu.VMEM((4, 32, 8, 128), F32),
            pltpu.VMEM((4, 32, 8, 128), F32),
            pltpu.VMEM((4, 32, 8, 128), F32),
            pltpu.VMEM((4, 32, 4, 8, 128), F32),
            pltpu.VMEM((4, 4, 8, 128), F32),
            pltpu.VMEM((32, 8, 128), F32),
            pltpu.VMEM((16, 16, 128), BF),
            pltpu.VMEM((16, 16, 128), BF),
            pltpu.VMEM((16, 2, 8, 128), F32),
            pltpu.VMEM((4, 256, 128), F32),
            pltpu.VMEM((2, 32, 8, 128), F32),
            pltpu.VMEM((2, 16, 2, 32, 128), BF),
            pltpu.VMEM((32, 2, 32, 128), BF),
            pltpu.SemaphoreType.DMA((2,)),
            pltpu.SemaphoreType.DMA((2,)),
            pltpu.SemaphoreType.DMA((2, 16)),
            pltpu.SemaphoreType.DMA((2, 16)),
            pltpu.SemaphoreType.DMA((2, 16)),
            pltpu.SemaphoreType.DMA((2, 16)),
            pltpu.SemaphoreType.DMA((16,)),
            pltpu.SemaphoreType.DMA((16,)),
            pltpu.SemaphoreType.DMA((9,)),
        ],
        compiler_params=pltpu.CompilerParams(
            collective_id=0, has_side_effects=True, vmem_limit_bytes=40 * 1024 * 1024
        ),
    )(*[pltpu.with_memory_space_constraint(value, pltpu.HBM) for value in operands])


def solution(mesh):
    in_specs = (P("mem", None, None, "lon"), P(), P(), P(), P(), P(), P(), P(), P())
    out_specs = P("mem", None, None, "lon")
    return jax.shard_map(
        on_device, mesh=mesh, in_specs=in_specs, out_specs=out_specs, check_vma=False
    )
```

```python
import math

import jax
import jax.numpy as jnp
from jax import lax
from jax.experimental import pallas as pl
from jax.experimental.pallas import tpu as pltpu
from jax.sharding import PartitionSpec as P

MESH = pl.DeviceIdType.MESH
HEADS = 4
BF = jnp.bfloat16
F32 = jnp.float32
PEERS = 16


def iota(shape, dim):
    return lax.broadcasted_iota(jnp.int32, shape, dim)


def ones_where(mask):
    return jnp.where(mask, 1.0, 0.0).astype(BF)


def dot(a, b, contract=((1,), (0,))):
    return lax.dot_general(a, b, (contract, ((), ())), preferred_element_type=F32)


def device(**where):
    return {name: index for name, index in where.items()}


def kernel(
    x_hbm,
    w1_hbm,
    w2_hbm,
    w3_hbm,
    gain_hbm,
    wq_hbm,
    wk_hbm,
    wv_hbm,
    wo_hbm,
    out_ref,
    x_ref,
    w1_ref,
    w2_ref,
    w3_ref,
    gain_ref,
    wq_ref,
    wk_ref,
    wv_ref,
    wo_ref,
    z_ref,
    xa_ref,
    xb_ref,
    xc_ref,
    band_ref,
    proj_ref,
    back_ref,
    gcol_ref,
    hs_ref,
    hr_ref,
    send_ref,
    recv_ref,
    q_ref,
    k_ref,
    v_ref,
    s_ref,
    mix_ref,
    ret_ref,
    got_ref,
    halo_send,
    halo_recv,
    go_send,
    go_recv,
    back_send,
    back_recv,
    load_sem,
):
    loads = [
        pltpu.make_async_copy(source, target, load_sem.at[index])
        for index, (source, target) in enumerate(
            (
                (x_hbm, x_ref),
                (w1_hbm, w1_ref),
                (w2_hbm, w2_ref),
                (w3_hbm, w3_ref),
                (gain_hbm, gain_ref),
                (wq_hbm, wq_ref),
                (wk_hbm, wk_ref),
                (wv_hbm, wv_ref),
                (wo_hbm, wo_ref),
            )
        )
    ]
    for load in loads:
        load.start()
    me = lax.axis_index("mem")
    col = lax.axis_index("lon")
    right, left = lax.rem(col + 1, PEERS), lax.rem(col + PEERS - 1, PEERS)

    barrier = pltpu.get_barrier_semaphore()

    def greet(step, carry):
        pl.semaphore_signal(
            barrier, inc=1, device_id={"mem": lax.rem(me + step, PEERS)}, device_id_type=MESH
        )
        return carry

    for side in (left, right):
        pl.semaphore_signal(barrier, inc=1, device_id={"lon": side}, device_id_type=MESH)
    lax.fori_loop(1, PEERS, greet, 0)

    for buf in (xa_ref, xb_ref, xc_ref):
        buf[0:64, :] = jnp.zeros((64, 384), BF)
        buf[1088:1152, :] = jnp.zeros((64, 384), BF)
    loads[0].wait()
    for m in range(2):
        z_ref[m] = x_ref[m].astype(F32).reshape(1024, 128)
        for lat in range(32):
            rows = z_ref[m, pl.ds(lat, 32, stride=32), :]
            xa_ref[64 + 32 * lat : 96 + 32 * lat, 128 * m : 128 * m + 128] = rows.astype(BF)

    r, lane = iota((32, 256), 0), iota((32, 256), 1)
    want = jnp.where(r < 16, 0, 120) + (r & 7) + jnp.where((r & 8) != 0, 128, 0)
    edges = dot(ones_where(lane == want), xa_ref[64:1088, 0:256], ((1,), (1,)))
    edges = edges.astype(BF)
    hs_ref[0] = edges[0:16]
    hs_ref[1] = edges[16:32]

    pl.semaphore_wait(barrier, PEERS + 1)

    def halo(side, target):
        return pltpu.make_async_remote_copy(
            src_ref=hs_ref.at[side],
            dst_ref=hr_ref.at[side],
            send_sem=halo_send.at[side],
            recv_sem=halo_recv.at[side],
            device_id={"lon": target},
            device_id_type=MESH,
        )

    to_left, to_right = halo(0, left), halo(1, right)
    to_left.start()
    to_right.start()

    for load in loads[1:]:
        load.wait()

    for layer, w_ref in enumerate((w1_ref, w2_ref, w3_ref)):
        for dx in range(5):
            pieces = [w_ref[dy, dx].astype(F32) for dy in range(5)]
            base = jnp.concatenate(pieces + [jnp.zeros((32, 96), F32)], axis=1)
            for up in range(4):
                rolled = base if up == 0 else pltpu.roll(base, 32 * up, 1)
                at = dx * 128 + up * 32
                band_ref[layer, at : at + 32, :] = rolled.astype(BF)

    def convolve(source, layer, block, tiles):
        rows = pl.ds(pl.multiple_of(block * 128, 128), 256)
        window = source[rows, 128 * tiles[0] : 128 * tiles[-1] + 128]
        total = [None] * len(tiles)
        for dx in range(5):
            y = dot(band_ref[layer, dx * 128 : dx * 128 + 128, :], window)
            for t in range(len(tiles)):
                part = y[:, 128 * t : 128 * t + 128]
                if dx != 2:
                    part = pltpu.roll(part, (2 - dx) % 128, 1)
                total[t] = part if total[t] is None else total[t] + part
        return total

    def silu_layer(source, target, layer, blocks, tiles):
        for block in blocks:
            total = convolve(source, layer, block, tiles)
            for t, value in zip(tiles, total):
                value = 0.5 * value
                value = value * jnp.tanh(value) + value
                at = 64 + 128 * block
                target[at : at + 128, 128 * t : 128 * t + 128] = value.astype(BF)

    def go(slot, peer):
        return pltpu.make_async_remote_copy(
            src_ref=send_ref.at[peer, slot],
            dst_ref=recv_ref.at[slot, me],
            send_sem=go_send.at[slot, peer],
            recv_sem=go_recv.at[slot, me],
            device_id={"mem": peer},
            device_id_type=MESH,
        )

    quarter = me // 4
    half, odd = quarter // 2, lax.rem(quarter, 2)
    order = (2 * (1 - half) + odd, 3 - 2 * half - odd, 2 * half + 1 - odd, quarter)

    def peers_of(step):
        first = 1 if step == 3 else 0
        return [4 * order[step] + lax.rem(me + row, 4) for row in range(first, 4)]

    def residual(block, t, total):
        at = pl.ds(pl.multiple_of(64 + block * 128, 64), 128)
        value = total + xa_ref[at, 128 * t : 128 * t + 128].astype(F32)
        return value.astype(BF)

    x_place, y_place, core = me // 8, lax.rem(me // 2, 4), lax.rem(me, 2)
    chips = [
        4 * lax.rem(x_place + across, 2) + lax.rem(y_place + along, 4)
        for across in (1, 0)
        for along in (2, 1, 3, 0)
    ]

    def send_chip(slot, step):
        if step == 7:
            recv_ref[slot, me] = send_ref[me, slot]
        else:
            go(slot, 2 * chips[step] + core).start()
        go(slot, 2 * chips[step] + 1 - core).start()

    silu_layer(xa_ref, xb_ref, 0, range(8), (0, 1))
    silu_layer(xb_ref, xc_ref, 1, range(8), (0, 1))
    lane = iota((32, 128), 1)
    for step in range(8):
        block = chips[step]
        total = convolve(xc_ref, 2, block, (0, 1))
        for m in range(2):
            state = residual(block, m, total[m]).astype(F32)
            for one in range(2):
                low, high = state[64 * one : 64 * one + 32], state[64 * one + 32 : 64 * one + 64]
                middle = jnp.where(lane < 64, pltpu.roll(low, 96, 1), pltpu.roll(high, 32, 1))
                outer = jnp.where(lane < 64, pltpu.roll(low, 32, 1), pltpu.roll(high, 96, 1))
                send_ref[2 * block + one, 0, m] = middle.astype(BF)
                send_ref[2 * block + one, 1, m] = outer.astype(BF)
        send_chip(0, step)

    to_left.wait()
    to_right.wait()

    r, lane = iota((256, 128), 0), iota((256, 128), 1)
    lon, base = r & 127, (r >> 7) * 64
    inner = jnp.where(lon < 16, base + 16 + lon, jnp.where(lon >= 112, base + lon - 80, -1))
    r2, lane2 = iota((32, 128), 0), iota((32, 128), 1)
    outer = jnp.where(r2 < 16, 48, 8) + (r2 & 7) + jnp.where((r2 & 8) != 0, 64, 0)
    strip = dot(xa_ref[64:1088, 0:256], ones_where(lane == inner))
    ring = hr_ref[...].reshape(32, 1024)
    strip = strip + dot(ring, ones_where(lane2 == outer), ((0,), (0,)))
    xa_ref[64:1088, 256:384] = strip.astype(BF)

    silu_layer(xa_ref, xb_ref, 0, range(8), (2,))
    silu_layer(xb_ref, xc_ref, 1, range(8), (2,))
    lane = iota((32, 128), 1)
    near = lane & 63
    inside = (near < 24) | (near >= 40)
    for step in range(8):
        block = chips[step]
        strip = residual(block, 2, convolve(xc_ref, 2, block, (2,))[0]).astype(F32)
        for m in range(2):
            for one in range(2):
                low, high = strip[64 * one : 64 * one + 32], strip[64 * one + 32 : 64 * one + 64]
                turns = [
                    pltpu.roll(part, (turn - 64 * m) % 128, 1)
                    for part, turn in ((low, -16), (low, 16), (high, 48), (high, 80))
                ]
                west = jnp.where(lane < 32, turns[0], turns[1])
                east = jnp.where(lane < 96, turns[2], turns[3])
                edge = jnp.where(lane < 64, west, east)
                main = send_ref[2 * block + one, 1, m].astype(F32)
                send_ref[2 * block + one, 1, m] = jnp.where(inside, main, edge).astype(BF)
        send_chip(1, step)

    r, c = iota((256, 32), 0), iota((256, 32), 1)
    spread = ones_where((r >> 3) == c)
    spread_out = ones_where((r & 31) == c)
    c, lane = iota((32, 256), 0), iota((32, 256), 1)
    tile = ones_where((lane & 31) == c)
    tile_out = ones_where((lane >> 3) == c)
    r, lane = iota((256, 256), 0), iota((256, 256), 1)
    own = (r & 7) == (lane >> 5)
    own_out = (r >> 5) == (lane & 7)
    for index, w_ref in enumerate((wq_ref, wk_ref, wv_ref)):
        tall = dot(spread, w_ref[...], ((1,), (1,))).astype(BF)
        full = jnp.where(own, dot(tall, tile), 0.0)
        proj_ref[256 * index : 256 * index + 256, :] = full.astype(BF)
    tall = dot(spread_out, wo_ref[...], ((1,), (1,))).astype(BF)
    back_ref[...] = jnp.where(own_out, dot(tall, tile_out), 0.0).astype(BF)
    eye = iota((32, 32), 0) == iota((32, 32), 1)
    gains = jnp.broadcast_to(gain_ref[...], (32, 32))
    gcol = jnp.sum(jnp.where(eye, gains, 0.0), axis=1, keepdims=True)
    gcol_ref[...] = jnp.broadcast_to(gcol, (32, 128))

    scale = math.log2(math.e) / math.sqrt(32 // HEADS)

    def back(slot, peer):
        return pltpu.make_async_remote_copy(
            src_ref=ret_ref.at[slot, peer],
            dst_ref=got_ref.at[slot, me],
            send_sem=back_send.at[slot, peer],
            recv_sem=back_recv.at[slot, me],
            device_id={"mem": peer},
            device_id_type=MESH,
        )

    def attend(slot, carry):
        for step in (3, 2, 0, 1):
            group = order[step]
            for peer in peers_of(step):
                pltpu.make_async_remote_copy(
                    src_ref=send_ref.at[peer, slot],
                    dst_ref=recv_ref.at[slot, peer],
                    send_sem=go_send.at[slot, peer],
                    recv_sem=go_recv.at[slot, peer],
                    device_id={"mem": peer},
                    device_id_type=MESH,
                ).wait_recv()
            values = recv_ref[slot, pl.ds(4 * group, 4)].astype(F32).reshape(8, 32, 128)
            centred = values - jnp.mean(values, axis=1, keepdims=True)
            spread = jnp.mean(centred * centred, axis=1, keepdims=True)
            normed = centred * lax.rsqrt(spread + 1e-05) * gcol_ref[...][None]
            out = dot(proj_ref[...], normed.astype(BF).reshape(256, 128))
            out = out.astype(BF).astype(F32)
            q_ref[group] = (out[0:256] * scale).reshape(32, 8, 128)
            k_ref[group] = out[256:512].reshape(32, 8, 128)
            v_ref[group] = out[512:768].reshape(32, 8, 128)

        for unit in ((0, 1), (2, 3)):
            count = len(unit)

            def head(h, carry):
                queries = [[q_ref[order[i], 8 * h + d] for i in unit] for d in range(8)]

                def score(group, peak):
                    peak = list(peak)
                    for n in range(8):
                        total = [None] * count
                        for d in range(8):
                            key = k_ref[group, 8 * h + d, pl.ds(n, 8, stride=0), :]
                            for i in range(count):
                                term = queries[d][i] * key
                                total[i] = term if d == 0 else total[i] + term
                        for i in range(count):
                            s_ref[8 * group + n, i] = total[i]
                            peak[i] = jnp.maximum(peak[i], total[i])
                    return tuple(peak)

                low = jnp.full((8, 128), -jnp.inf, F32)
                peak = lax.fori_loop(0, 4, score, (low,) * count, unroll=4)

                def mix(group, state):
                    weight, mixed = list(state[0]), [list(m) for m in state[1]]
                    for n in range(8):
                        probs = [jnp.exp2(s_ref[8 * group + n, i] - peak[i]) for i in range(count)]
                        for i in range(count):
                            weight[i] = weight[i] + probs[i]
                        for d in range(8):
                            value = v_ref[group, 8 * h + d, pl.ds(n, 8, stride=0), :]
                            for i in range(count):
                                mixed[d][i] = mixed[d][i] + probs[i] * value
                    return tuple(weight), tuple(tuple(m) for m in mixed)

                zero = jnp.zeros((8, 128), F32)
                start = ((zero,) * count, ((zero,) * count,) * 8)
                weight, mixed = lax.fori_loop(0, 4, mix, start, unroll=4)
                for i in range(count):
                    inverse = 1.0 / weight[i]
                    for d in range(8):
                        mix_ref[i, 8 * h + d] = mixed[d][i] * inverse
                return carry

            lax.fori_loop(0, HEADS, head, 0)

            for i, step in enumerate(unit):
                group = order[step]
                mixed = mix_ref[i].reshape(256, 128).astype(BF)
                state = recv_ref[slot, pl.ds(4 * group, 4)].astype(F32).reshape(256, 128)
                final = dot(back_ref[...], mixed) + state
                ret_ref[slot, pl.ds(4 * group, 4)] = final.astype(BF).reshape(4, 2, 32, 128)
                if step == 3:
                    got_ref[slot, me] = ret_ref[slot, me]
                for peer in peers_of(step):
                    back(slot, peer).start()
        return carry

    lax.fori_loop(0, 2, attend, 0)

    def sent(step, carry):
        peer = lax.rem(me + step, PEERS)
        go(0, peer).wait_send()
        go(1, peer).wait_send()
        back(0, peer).wait_send()
        return carry

    lax.fori_loop(1, PEERS, sent, 0)

    lane = iota((32, 128), 1)
    middle = (lane >= 32) & (lane < 96)
    for step in range(4):
        for slot in range(2):
            for peer in peers_of(step):
                pltpu.make_async_remote_copy(
                    src_ref=ret_ref.at[slot, peer],
                    dst_ref=got_ref.at[slot, peer],
                    send_sem=back_send.at[slot, peer],
                    recv_sem=back_recv.at[slot, peer],
                    device_id={"mem": peer},
                    device_id_type=MESH,
                ).wait_recv()
        for row in range(4):
            peer = 4 * order[step] + row
            for m in range(2):
                inner, outer = got_ref[0, peer, m].astype(F32), got_ref[1, peer, m].astype(F32)
                low = jnp.where(middle, pltpu.roll(inner, 32, 1), pltpu.roll(outer, 96, 1))
                high = jnp.where(middle, pltpu.roll(inner, 96, 1), pltpu.roll(outer, 32, 1))
                z_ref[m, pl.ds(2 * peer, 32, stride=32), :] = low
                z_ref[m, pl.ds(2 * peer + 1, 32, stride=32), :] = high

    for m in range(2):
        out_ref[m] = z_ref[m].astype(BF).reshape(32, 32, 128)

    for step in range(4):
        for peer in peers_of(step):
            back(1, peer).wait_send()


def on_device(members, conv_one, conv_two, conv_three, norm_gain, w_query, w_key, w_value, w_out):
    taps = [jnp.transpose(w, (2, 3, 0, 1)) for w in (conv_one, conv_two, conv_three)]
    vmem = pl.BlockSpec(memory_space=pltpu.VMEM)
    operands = (members, *taps, norm_gain.reshape(1, 32), w_query, w_key, w_value, w_out)
    return pl.pallas_call(
        kernel,
        out_shape=jax.ShapeDtypeStruct(members.shape, BF),
        in_specs=[pl.BlockSpec(memory_space=pltpu.HBM)] * 9,
        out_specs=vmem,
        scratch_shapes=[
            pltpu.VMEM((2, 32, 32, 128), BF),
            pltpu.VMEM((5, 5, 32, 32), BF),
            pltpu.VMEM((5, 5, 32, 32), BF),
            pltpu.VMEM((5, 5, 32, 32), BF),
            pltpu.VMEM((1, 32), F32),
            pltpu.VMEM((32, 32), BF),
            pltpu.VMEM((32, 32), BF),
            pltpu.VMEM((32, 32), BF),
            pltpu.VMEM((32, 32), BF),
            pltpu.VMEM((2, 1024, 128), F32),
            pltpu.VMEM((1152, 384), BF),
            pltpu.VMEM((1152, 384), BF),
            pltpu.VMEM((1152, 384), BF),
            pltpu.VMEM((3, 640, 256), BF),
            pltpu.VMEM((768, 256), BF),
            pltpu.VMEM((256, 256), BF),
            pltpu.VMEM((32, 128), F32),
            pltpu.VMEM((2, 16, 1024), BF),
            pltpu.VMEM((2, 16, 1024), BF),
            pltpu.VMEM((16, 2, 2, 32, 128), BF),
            pltpu.VMEM((2, 16, 2, 32, 128), BF),
            pltpu.VMEM((4, 32, 8, 128), F32),
            pltpu.VMEM((4, 32, 8, 128), F32),
            pltpu.VMEM((4, 32, 8, 128), F32),
            pltpu.VMEM((32, 4, 8, 128), F32),
            pltpu.VMEM((4, 32, 8, 128), F32),
            pltpu.VMEM((2, 16, 2, 32, 128), BF),
            pltpu.VMEM((2, 16, 2, 32, 128), BF),
            pltpu.SemaphoreType.DMA((2,)),
            pltpu.SemaphoreType.DMA((2,)),
            pltpu.SemaphoreType.DMA((2, 16)),
            pltpu.SemaphoreType.DMA((2, 16)),
            pltpu.SemaphoreType.DMA((2, 16)),
            pltpu.SemaphoreType.DMA((2, 16)),
            pltpu.SemaphoreType.DMA((9,)),
        ],
        compiler_params=pltpu.CompilerParams(
            collective_id=0, has_side_effects=True, vmem_limit_bytes=40 * 1024 * 1024
        ),
    )(*[pltpu.with_memory_space_constraint(value, pltpu.HBM) for value in operands])


def solution(mesh):
    in_specs = (P("mem", None, None, "lon"), P(), P(), P(), P(), P(), P(), P(), P())
    out_specs = P("mem", None, None, "lon")
    return jax.shard_map(
        on_device, mesh=mesh, in_specs=in_specs, out_specs=out_specs, check_vma=False
    )
```

```python
import math

import jax
import jax.numpy as jnp
from jax import lax
from jax.experimental import pallas as pl
from jax.experimental.pallas import tpu as pltpu
from jax.sharding import PartitionSpec as P

MESH = pl.DeviceIdType.MESH
HEADS = 4
BF = jnp.bfloat16
F32 = jnp.float32
PEERS = 16


def iota(shape, dim):
    return lax.broadcasted_iota(jnp.int32, shape, dim)


def ones_where(mask):
    return jnp.where(mask, 1.0, 0.0).astype(BF)


def dot(a, b, contract=((1,), (0,))):
    return lax.dot_general(a, b, (contract, ((), ())), preferred_element_type=F32)


def device(**where):
    return {name: index for name, index in where.items()}


def kernel(
    x_hbm,
    w1_hbm,
    w2_hbm,
    w3_hbm,
    gain_hbm,
    wq_hbm,
    wk_hbm,
    wv_hbm,
    wo_hbm,
    out_ref,
    x_ref,
    w1_ref,
    w2_ref,
    w3_ref,
    gain_ref,
    wq_ref,
    wk_ref,
    wv_ref,
    wo_ref,
    z_ref,
    xa_ref,
    xb_ref,
    xc_ref,
    band_ref,
    proj_ref,
    back_ref,
    gcol_ref,
    hs_ref,
    hr_ref,
    send_ref,
    recv_ref,
    q_ref,
    k_ref,
    v_ref,
    s_ref,
    mix_ref,
    ret_ref,
    got_ref,
    halo_send,
    halo_recv,
    go_send,
    go_recv,
    back_send,
    back_recv,
    load_sem,
):
    loads = [
        pltpu.make_async_copy(source, target, load_sem.at[index])
        for index, (source, target) in enumerate(
            (
                (x_hbm, x_ref),
                (w1_hbm, w1_ref),
                (w2_hbm, w2_ref),
                (w3_hbm, w3_ref),
                (gain_hbm, gain_ref),
                (wq_hbm, wq_ref),
                (wk_hbm, wk_ref),
                (wv_hbm, wv_ref),
                (wo_hbm, wo_ref),
            )
        )
    ]
    for load in loads:
        load.start()
    me = lax.axis_index("mem")
    col = lax.axis_index("lon")
    right, left = lax.rem(col + 1, PEERS), lax.rem(col + PEERS - 1, PEERS)

    barrier = pltpu.get_barrier_semaphore()

    def greet(step, carry):
        pl.semaphore_signal(
            barrier, inc=1, device_id={"mem": lax.rem(me + step, PEERS)}, device_id_type=MESH
        )
        return carry

    for side in (left, right):
        pl.semaphore_signal(barrier, inc=1, device_id={"lon": side}, device_id_type=MESH)
    lax.fori_loop(1, PEERS, greet, 0)

    for buf in (xa_ref, xb_ref, xc_ref):
        buf[:, 0:64, :] = jnp.zeros((5, 64, 384), BF)
        buf[:, 1088:1152, :] = jnp.zeros((5, 64, 384), BF)
    loads[0].wait()
    for m in range(2):
        z_ref[m] = x_ref[m].astype(F32).reshape(1024, 128)
        for lat in range(32):
            rows = z_ref[m, pl.ds(lat, 32, stride=32), :]
            xa_ref[2, 64 + 32 * lat : 96 + 32 * lat, 128 * m : 128 * m + 128] = rows.astype(BF)

    r, lane = iota((32, 256), 0), iota((32, 256), 1)
    want = jnp.where(r < 16, 0, 120) + (r & 7) + jnp.where((r & 8) != 0, 128, 0)
    edges = dot(ones_where(lane == want), xa_ref[2, 64:1088, 0:256], ((1,), (1,)))
    edges = edges.astype(BF)
    hs_ref[0] = edges[0:16]
    hs_ref[1] = edges[16:32]

    for load in loads[1:]:
        load.wait()

    for layer, w_ref in enumerate((w1_ref, w2_ref, w3_ref)):
        for dx in range(5):
            pieces = [w_ref[dy, dx].astype(F32) for dy in range(5)]
            base = jnp.concatenate(pieces + [jnp.zeros((32, 96), F32)], axis=1)
            for up in range(4):
                rolled = base if up == 0 else pltpu.roll(base, 32 * up, 1)
                columns = slice(256 * dx, 256 * dx + 256)
                band_ref[layer, 32 * up : 32 * up + 32, columns] = rolled.astype(BF)

    def spread_columns(target, rows, t, value):
        columns = slice(128 * t, 128 * t + 128)
        for dx in range(5):
            turned = value if dx == 2 else pltpu.roll(value, (2 - dx) % 128, 1)
            target[dx, rows, columns] = turned

    def convolve(source, layer, parts):
        windows = []
        for block, t in parts:
            rows = pl.ds(pl.multiple_of(block * 128, 128), 256)
            columns = slice(128 * t, 128 * t + 128)
            windows.append(
                jnp.concatenate([source[dx, rows, columns] for dx in range(5)], axis=0)
            )
        y = dot(band_ref[layer], jnp.concatenate(windows, axis=1))
        return [y[:, 128 * i : 128 * i + 128] for i in range(len(parts))]

    def silu_layer(source, target, layer, pieces):
        for parts in pieces:
            for (block, t), value in zip(parts, convolve(source, layer, parts)):
                value = 0.5 * value
                value = value * jnp.tanh(value) + value
                at = 64 + 128 * block
                spread_columns(target, slice(at, at + 128), t, value.astype(BF))

    own = [((block, 0), (block, 1)) for block in range(8)]
    strips = [((block, 2), (block + 1, 2)) for block in range(0, 8, 2)]

    for t in range(2):
        spread_columns(xa_ref, slice(64, 1088), t, xa_ref[2, 64:1088, 128 * t : 128 * t + 128])
    silu_layer(xa_ref, xb_ref, 0, own[:4])

    pl.semaphore_wait(barrier, PEERS + 1)

    def halo(side, target):
        return pltpu.make_async_remote_copy(
            src_ref=hs_ref.at[side],
            dst_ref=hr_ref.at[side],
            send_sem=halo_send.at[side],
            recv_sem=halo_recv.at[side],
            device_id={"lon": target},
            device_id_type=MESH,
        )

    to_left, to_right = halo(0, left), halo(1, right)
    to_left.start()
    to_right.start()

    def go(slot, peer):
        return pltpu.make_async_remote_copy(
            src_ref=send_ref.at[peer, slot],
            dst_ref=recv_ref.at[slot, me],
            send_sem=go_send.at[slot, peer],
            recv_sem=go_recv.at[slot, me],
            device_id={"mem": peer},
            device_id_type=MESH,
        )

    quarter = me // 4
    half, odd = quarter // 2, lax.rem(quarter, 2)
    order = (2 * (1 - half) + odd, 3 - 2 * half - odd, 2 * half + 1 - odd, quarter)

    def peers_of(step):
        first = 1 if step == 3 else 0
        return [4 * order[step] + lax.rem(me + row, 4) for row in range(first, 4)]

    def residual(block, t, total):
        at = pl.ds(pl.multiple_of(64 + block * 128, 64), 128)
        value = total + xa_ref[2, at, 128 * t : 128 * t + 128].astype(F32)
        return value.astype(BF)

    x_place, y_place, core = me // 8, lax.rem(me // 2, 4), lax.rem(me, 2)
    chips = [
        4 * lax.rem(x_place + across, 2) + lax.rem(y_place + along, 4)
        for across in (1, 0)
        for along in (2, 1, 3, 0)
    ]

    def send_chip(slot, step):
        if step == 7:
            recv_ref[slot, me] = send_ref[me, slot]
        else:
            go(slot, 2 * chips[step] + core).start()
        go(slot, 2 * chips[step] + 1 - core).start()

    silu_layer(xa_ref, xb_ref, 0, own[4:])
    silu_layer(xb_ref, xc_ref, 1, own)
    lane = iota((32, 128), 1)
    for step in range(8):
        block = chips[step]
        total = convolve(xc_ref, 2, ((block, 0), (block, 1)))
        for m in range(2):
            state = residual(block, m, total[m]).astype(F32)
            for one in range(2):
                low, high = state[64 * one : 64 * one + 32], state[64 * one + 32 : 64 * one + 64]
                middle = jnp.where(lane < 64, pltpu.roll(low, 96, 1), pltpu.roll(high, 32, 1))
                outer = jnp.where(lane < 64, pltpu.roll(low, 32, 1), pltpu.roll(high, 96, 1))
                send_ref[2 * block + one, 0, m] = middle.astype(BF)
                send_ref[2 * block + one, 1, m] = outer.astype(BF)
        send_chip(0, step)

    to_left.wait()
    to_right.wait()

    r, lane = iota((256, 128), 0), iota((256, 128), 1)
    lon, base = r & 127, (r >> 7) * 64
    inner = jnp.where(lon < 16, base + 16 + lon, jnp.where(lon >= 112, base + lon - 80, -1))
    r2, lane2 = iota((32, 128), 0), iota((32, 128), 1)
    outer = jnp.where(r2 < 16, 48, 8) + (r2 & 7) + jnp.where((r2 & 8) != 0, 64, 0)
    strip = dot(xa_ref[2, 64:1088, 0:256], ones_where(lane == inner))
    ring = hr_ref[...].reshape(32, 1024)
    strip = strip + dot(ring, ones_where(lane2 == outer), ((0,), (0,)))
    spread_columns(xa_ref, slice(64, 1088), 2, strip.astype(BF))

    silu_layer(xa_ref, xb_ref, 0, strips)
    silu_layer(xb_ref, xc_ref, 1, strips)
    lane = iota((32, 128), 1)
    near = lane & 63
    inside = (near < 24) | (near >= 40)
    for step in range(8):
        block = chips[step]
        if step % 2 == 0:
            both = convolve(xc_ref, 2, ((block, 2), (chips[step + 1], 2)))
        strip = residual(block, 2, both[step % 2]).astype(F32)
        for m in range(2):
            for one in range(2):
                low, high = strip[64 * one : 64 * one + 32], strip[64 * one + 32 : 64 * one + 64]
                turns = [
                    pltpu.roll(part, (turn - 64 * m) % 128, 1)
                    for part, turn in ((low, -16), (low, 16), (high, 48), (high, 80))
                ]
                west = jnp.where(lane < 32, turns[0], turns[1])
                east = jnp.where(lane < 96, turns[2], turns[3])
                edge = jnp.where(lane < 64, west, east)
                main = send_ref[2 * block + one, 1, m].astype(F32)
                send_ref[2 * block + one, 1, m] = jnp.where(inside, main, edge).astype(BF)
        send_chip(1, step)

    r, c = iota((256, 32), 0), iota((256, 32), 1)
    spread = ones_where((r >> 3) == c)
    spread_out = ones_where((r & 31) == c)
    c, lane = iota((32, 256), 0), iota((32, 256), 1)
    tile = ones_where((lane & 31) == c)
    tile_out = ones_where((lane >> 3) == c)
    r, lane = iota((256, 256), 0), iota((256, 256), 1)
    same = (r & 7) == (lane >> 5)
    same_out = (r >> 5) == (lane & 7)
    for index, w_ref in enumerate((wq_ref, wk_ref, wv_ref)):
        tall = dot(spread, w_ref[...], ((1,), (1,))).astype(BF)
        full = jnp.where(same, dot(tall, tile), 0.0)
        proj_ref[256 * index : 256 * index + 256, :] = full.astype(BF)
    tall = dot(spread_out, wo_ref[...], ((1,), (1,))).astype(BF)
    back_ref[...] = jnp.where(same_out, dot(tall, tile_out), 0.0).astype(BF)
    eye = iota((32, 32), 0) == iota((32, 32), 1)
    gains = jnp.broadcast_to(gain_ref[...], (32, 32))
    gcol = jnp.sum(jnp.where(eye, gains, 0.0), axis=1, keepdims=True)
    gcol_ref[...] = jnp.broadcast_to(gcol, (32, 128))

    scale = math.log2(math.e) / math.sqrt(32 // HEADS)

    def back(slot, peer):
        return pltpu.make_async_remote_copy(
            src_ref=ret_ref.at[slot, peer],
            dst_ref=got_ref.at[slot, me],
            send_sem=back_send.at[slot, peer],
            recv_sem=back_recv.at[slot, me],
            device_id={"mem": peer},
            device_id_type=MESH,
        )

    def attend(slot, carry):
        for step in (3, 2, 0, 1):
            group = order[step]
            for peer in peers_of(step):
                pltpu.make_async_remote_copy(
                    src_ref=send_ref.at[peer, slot],
                    dst_ref=recv_ref.at[slot, peer],
                    send_sem=go_send.at[slot, peer],
                    recv_sem=go_recv.at[slot, peer],
                    device_id={"mem": peer},
                    device_id_type=MESH,
                ).wait_recv()
            values = recv_ref[slot, pl.ds(4 * group, 4)].astype(F32).reshape(8, 32, 128)
            centred = values - jnp.mean(values, axis=1, keepdims=True)
            spread = jnp.mean(centred * centred, axis=1, keepdims=True)
            normed = centred * lax.rsqrt(spread + 1e-05) * gcol_ref[...][None]
            out = dot(proj_ref[...], normed.astype(BF).reshape(256, 128))
            out = out.astype(BF).astype(F32)
            q_ref[group] = (out[0:256] * scale).reshape(32, 8, 128)
            k_ref[group] = out[256:512].reshape(32, 8, 128)
            v_ref[group] = out[512:768].reshape(32, 8, 128)

        for unit in ((0, 1), (2, 3)):
            count = len(unit)

            def head(h, carry):
                queries = [[q_ref[order[i], 8 * h + d] for i in unit] for d in range(8)]

                def score(group, peak):
                    peak = list(peak)
                    for n in range(8):
                        total = [None] * count
                        for d in range(8):
                            key = k_ref[group, 8 * h + d, pl.ds(n, 8, stride=0), :]
                            for i in range(count):
                                term = queries[d][i] * key
                                total[i] = term if d == 0 else total[i] + term
                        for i in range(count):
                            s_ref[8 * group + n, i] = total[i]
                            peak[i] = jnp.maximum(peak[i], total[i])
                    return tuple(peak)

                low = jnp.full((8, 128), -jnp.inf, F32)
                peak = lax.fori_loop(0, 4, score, (low,) * count, unroll=4)

                def mix(group, state):
                    weight, mixed = list(state[0]), [list(m) for m in state[1]]
                    for n in range(8):
                        probs = [jnp.exp2(s_ref[8 * group + n, i] - peak[i]) for i in range(count)]
                        for i in range(count):
                            weight[i] = weight[i] + probs[i]
                        for d in range(8):
                            value = v_ref[group, 8 * h + d, pl.ds(n, 8, stride=0), :]
                            for i in range(count):
                                mixed[d][i] = mixed[d][i] + probs[i] * value
                    return tuple(weight), tuple(tuple(m) for m in mixed)

                zero = jnp.zeros((8, 128), F32)
                start = ((zero,) * count, ((zero,) * count,) * 8)
                weight, mixed = lax.fori_loop(0, 4, mix, start, unroll=4)
                for i in range(count):
                    inverse = 1.0 / weight[i]
                    for d in range(8):
                        mix_ref[i, 8 * h + d] = mixed[d][i] * inverse
                return carry

            lax.fori_loop(0, HEADS, head, 0)

            for i, step in enumerate(unit):
                group = order[step]
                mixed = mix_ref[i].reshape(256, 128).astype(BF)
                state = recv_ref[slot, pl.ds(4 * group, 4)].astype(F32).reshape(256, 128)
                final = dot(back_ref[...], mixed) + state
                ret_ref[slot, pl.ds(4 * group, 4)] = final.astype(BF).reshape(4, 2, 32, 128)
                if step == 3:
                    got_ref[slot, me] = ret_ref[slot, me]
                for peer in peers_of(step):
                    back(slot, peer).start()
        return carry

    lax.fori_loop(0, 2, attend, 0)

    def sent(step, carry):
        peer = lax.rem(me + step, PEERS)
        go(0, peer).wait_send()
        go(1, peer).wait_send()
        back(0, peer).wait_send()
        return carry

    lax.fori_loop(1, PEERS, sent, 0)

    lane = iota((32, 128), 1)
    middle = (lane >= 32) & (lane < 96)
    for step in range(4):
        for slot in range(2):
            for peer in peers_of(step):
                pltpu.make_async_remote_copy(
                    src_ref=ret_ref.at[slot, peer],
                    dst_ref=got_ref.at[slot, peer],
                    send_sem=back_send.at[slot, peer],
                    recv_sem=back_recv.at[slot, peer],
                    device_id={"mem": peer},
                    device_id_type=MESH,
                ).wait_recv()
        for row in range(4):
            peer = 4 * order[step] + row
            for m in range(2):
                inner, outer = got_ref[0, peer, m].astype(F32), got_ref[1, peer, m].astype(F32)
                low = jnp.where(middle, pltpu.roll(inner, 32, 1), pltpu.roll(outer, 96, 1))
                high = jnp.where(middle, pltpu.roll(inner, 96, 1), pltpu.roll(outer, 32, 1))
                z_ref[m, pl.ds(2 * peer, 32, stride=32), :] = low
                z_ref[m, pl.ds(2 * peer + 1, 32, stride=32), :] = high

    for m in range(2):
        out_ref[m] = z_ref[m].astype(BF).reshape(32, 32, 128)

    for step in range(4):
        for peer in peers_of(step):
            back(1, peer).wait_send()


def on_device(members, conv_one, conv_two, conv_three, norm_gain, w_query, w_key, w_value, w_out):
    taps = [jnp.transpose(w, (2, 3, 0, 1)) for w in (conv_one, conv_two, conv_three)]
    vmem = pl.BlockSpec(memory_space=pltpu.VMEM)
    operands = (members, *taps, norm_gain.reshape(1, 32), w_query, w_key, w_value, w_out)
    return pl.pallas_call(
        kernel,
        out_shape=jax.ShapeDtypeStruct(members.shape, BF),
        in_specs=[pl.BlockSpec(memory_space=pltpu.HBM)] * 9,
        out_specs=vmem,
        scratch_shapes=[
            pltpu.VMEM((2, 32, 32, 128), BF),
            pltpu.VMEM((5, 5, 32, 32), BF),
            pltpu.VMEM((5, 5, 32, 32), BF),
            pltpu.VMEM((5, 5, 32, 32), BF),
            pltpu.VMEM((1, 32), F32),
            pltpu.VMEM((32, 32), BF),
            pltpu.VMEM((32, 32), BF),
            pltpu.VMEM((32, 32), BF),
            pltpu.VMEM((32, 32), BF),
            pltpu.VMEM((2, 1024, 128), F32),
            pltpu.VMEM((5, 1152, 384), BF),
            pltpu.VMEM((5, 1152, 384), BF),
            pltpu.VMEM((5, 1152, 384), BF),
            pltpu.VMEM((3, 128, 1280), BF),
            pltpu.VMEM((768, 256), BF),
            pltpu.VMEM((256, 256), BF),
            pltpu.VMEM((32, 128), F32),
            pltpu.VMEM((2, 16, 1024), BF),
            pltpu.VMEM((2, 16, 1024), BF),
            pltpu.VMEM((16, 2, 2, 32, 128), BF),
            pltpu.VMEM((2, 16, 2, 32, 128), BF),
            pltpu.VMEM((4, 32, 8, 128), F32),
            pltpu.VMEM((4, 32, 8, 128), F32),
            pltpu.VMEM((4, 32, 8, 128), F32),
            pltpu.VMEM((32, 4, 8, 128), F32),
            pltpu.VMEM((4, 32, 8, 128), F32),
            pltpu.VMEM((2, 16, 2, 32, 128), BF),
            pltpu.VMEM((2, 16, 2, 32, 128), BF),
            pltpu.SemaphoreType.DMA((2,)),
            pltpu.SemaphoreType.DMA((2,)),
            pltpu.SemaphoreType.DMA((2, 16)),
            pltpu.SemaphoreType.DMA((2, 16)),
            pltpu.SemaphoreType.DMA((2, 16)),
            pltpu.SemaphoreType.DMA((2, 16)),
            pltpu.SemaphoreType.DMA((9,)),
        ],
        compiler_params=pltpu.CompilerParams(
            collective_id=0, has_side_effects=True, vmem_limit_bytes=40 * 1024 * 1024
        ),
    )(*[pltpu.with_memory_space_constraint(value, pltpu.HBM) for value in operands])


def solution(mesh):
    in_specs = (P("mem", None, None, "lon"), P(), P(), P(), P(), P(), P(), P(), P())
    out_specs = P("mem", None, None, "lon")
    return jax.shard_map(
        on_device, mesh=mesh, in_specs=in_specs, out_specs=out_specs, check_vma=False
    )
```

```python
import math

import jax
import jax.numpy as jnp
from jax import lax
from jax.experimental import pallas as pl
from jax.experimental.pallas import tpu as pltpu
from jax.sharding import PartitionSpec as P

MESH = pl.DeviceIdType.MESH
HEADS = 4
BF = jnp.bfloat16
F32 = jnp.float32
PEERS = 16


def iota(shape, dim):
    return lax.broadcasted_iota(jnp.int32, shape, dim)


def ones_where(mask):
    return jnp.where(mask, 1.0, 0.0).astype(BF)


def dot(a, b, contract=((1,), (0,))):
    return lax.dot_general(a, b, (contract, ((), ())), preferred_element_type=F32)


def device(**where):
    return {name: index for name, index in where.items()}


def kernel(
    x_hbm,
    w1_hbm,
    w2_hbm,
    w3_hbm,
    gain_hbm,
    wq_hbm,
    wk_hbm,
    wv_hbm,
    wo_hbm,
    out_ref,
    x_ref,
    w1_ref,
    w2_ref,
    w3_ref,
    gain_ref,
    wq_ref,
    wk_ref,
    wv_ref,
    wo_ref,
    z_ref,
    xa_ref,
    xb_ref,
    xc_ref,
    band_ref,
    proj_ref,
    back_ref,
    gcol_ref,
    hs_ref,
    hr_ref,
    send_ref,
    recv_ref,
    q_ref,
    k_ref,
    v_ref,
    s_ref,
    mix_ref,
    ret_ref,
    got_ref,
    strip_ref,
    halo_send,
    halo_recv,
    go_send,
    go_recv,
    back_send,
    back_recv,
    load_sem,
):
    loads = [
        pltpu.make_async_copy(source, target, load_sem.at[index])
        for index, (source, target) in enumerate(
            (
                (x_hbm.at[0], x_ref.at[0]),
                (x_hbm.at[1], x_ref.at[1]),
                (w1_hbm, w1_ref),
                (w2_hbm, w2_ref),
                (w3_hbm, w3_ref),
                (gain_hbm, gain_ref),
                (wq_hbm, wq_ref),
                (wk_hbm, wk_ref),
                (wv_hbm, wv_ref),
                (wo_hbm, wo_ref),
            )
        )
    ]
    for load in loads:
        load.start()
    me = lax.axis_index("mem")
    col = lax.axis_index("lon")
    right, left = lax.rem(col + 1, PEERS), lax.rem(col + PEERS - 1, PEERS)

    barrier = pltpu.get_barrier_semaphore()

    def greet(step, carry):
        pl.semaphore_signal(
            barrier, inc=1, device_id={"mem": lax.rem(me + step, PEERS)}, device_id_type=MESH
        )
        return carry

    for side in (left, right):
        pl.semaphore_signal(barrier, inc=1, device_id={"lon": side}, device_id_type=MESH)
    lax.fori_loop(1, PEERS, greet, 0)

    for buf in (xa_ref, xb_ref, xc_ref):
        buf[:, 0:64, :] = jnp.zeros((5, 64, 384), BF)
        buf[:, 1088:1152, :] = jnp.zeros((5, 64, 384), BF)
    for m in range(2):
        loads[m].wait()
        z_ref[m] = x_ref[m].astype(F32).reshape(1024, 128)
        for lat in range(32):
            rows = z_ref[m, pl.ds(lat, 32, stride=32), :]
            xa_ref[2, 64 + 32 * lat : 96 + 32 * lat, 128 * m : 128 * m + 128] = rows.astype(BF)

    r, lane = iota((32, 256), 0), iota((32, 256), 1)
    want = jnp.where(r < 16, 0, 120) + (r & 7) + jnp.where((r & 8) != 0, 128, 0)
    edges = dot(ones_where(lane == want), xa_ref[2, 64:1088, 0:256], ((1,), (1,)))
    edges = edges.astype(BF)
    hs_ref[0] = edges[0:16]
    hs_ref[1] = edges[16:32]

    for load in loads[2:]:
        load.wait()

    for layer, w_ref in enumerate((w1_ref, w2_ref, w3_ref)):
        for dx in range(5):
            pieces = [w_ref[dy, dx].astype(F32) for dy in range(5)]
            base = jnp.concatenate(pieces + [jnp.zeros((32, 96), F32)], axis=1)
            for up in range(4):
                rolled = base if up == 0 else pltpu.roll(base, 32 * up, 1)
                columns = slice(256 * dx, 256 * dx + 256)
                band_ref[layer, 32 * up : 32 * up + 32, columns] = rolled.astype(BF)

    def spread_columns(target, rows, t, value):
        columns = slice(128 * t, 128 * t + 128)
        for dx in range(5):
            turned = value if dx == 2 else pltpu.roll(value, (2 - dx) % 128, 1)
            target[dx, rows, columns] = turned

    def convolve(source, layer, parts):
        windows = []
        for block, t in parts:
            rows = pl.ds(pl.multiple_of(block * 128, 128), 256)
            columns = slice(128 * t, 128 * t + 128)
            windows.append(
                jnp.concatenate([source[dx, rows, columns] for dx in range(5)], axis=0)
            )
        y = dot(band_ref[layer], jnp.concatenate(windows, axis=1))
        return [y[:, 128 * i : 128 * i + 128] for i in range(len(parts))]

    def silu_layer(source, target, layer, pieces):
        for parts in pieces:
            for (block, t), value in zip(parts, convolve(source, layer, parts)):
                value = 0.5 * value
                value = value * jnp.tanh(value) + value
                at = 64 + 128 * block
                spread_columns(target, slice(at, at + 128), t, value.astype(BF))

    own = [((block, 0), (block, 1)) for block in range(8)]
    strips = [((block, 2), (block + 1, 2)) for block in range(0, 8, 2)]

    for t in range(2):
        spread_columns(xa_ref, slice(64, 1088), t, xa_ref[2, 64:1088, 128 * t : 128 * t + 128])
    silu_layer(xa_ref, xb_ref, 0, own[:4])

    pl.semaphore_wait(barrier, PEERS + 1)

    def halo(side, target):
        return pltpu.make_async_remote_copy(
            src_ref=hs_ref.at[side],
            dst_ref=hr_ref.at[side],
            send_sem=halo_send.at[side],
            recv_sem=halo_recv.at[side],
            device_id={"lon": target},
            device_id_type=MESH,
        )

    to_left, to_right = halo(0, left), halo(1, right)
    to_left.start()
    to_right.start()

    def go(slot, peer):
        return pltpu.make_async_remote_copy(
            src_ref=send_ref.at[peer, slot],
            dst_ref=recv_ref.at[slot, me],
            send_sem=go_send.at[slot, peer],
            recv_sem=go_recv.at[slot, me],
            device_id={"mem": peer},
            device_id_type=MESH,
        )

    quarter = me // 4
    half, odd = quarter // 2, lax.rem(quarter, 2)
    order = (2 * (1 - half) + odd, 3 - 2 * half - odd, 2 * half + 1 - odd, quarter)

    def peers_of(step):
        first = 1 if step == 3 else 0
        return [4 * order[step] + lax.rem(me + row, 4) for row in range(first, 4)]

    def residual(block, t, total):
        at = pl.ds(pl.multiple_of(64 + block * 128, 64), 128)
        value = total + xa_ref[2, at, 128 * t : 128 * t + 128].astype(F32)
        return value.astype(BF)

    x_place, y_place, core = me // 8, lax.rem(me // 2, 4), lax.rem(me, 2)
    chips = [
        4 * lax.rem(x_place + across, 2) + lax.rem(y_place + along, 4)
        for across in (1, 0)
        for along in (2, 1, 3, 0)
    ]

    def send_chip(slot, step):
        if step == 7:
            recv_ref[slot, me] = send_ref[me, slot]
        else:
            go(slot, 2 * chips[step] + core).start()
        go(slot, 2 * chips[step] + 1 - core).start()

    silu_layer(xa_ref, xb_ref, 0, own[4:])
    silu_layer(xb_ref, xc_ref, 1, own)
    lane = iota((32, 128), 1)
    for step in range(8):
        block = chips[step]
        total = convolve(xc_ref, 2, ((block, 0), (block, 1)))
        for m in range(2):
            state = residual(block, m, total[m]).astype(F32)
            for one in range(2):
                low, high = state[64 * one : 64 * one + 32], state[64 * one + 32 : 64 * one + 64]
                middle = jnp.where(lane < 64, pltpu.roll(low, 96, 1), pltpu.roll(high, 32, 1))
                outer = jnp.where(lane < 64, pltpu.roll(low, 32, 1), pltpu.roll(high, 96, 1))
                send_ref[2 * block + one, 0, m] = middle.astype(BF)
                send_ref[2 * block + one, 1, m] = outer.astype(BF)
        send_chip(0, step)

    r, c = iota((256, 32), 0), iota((256, 32), 1)
    spread = ones_where((r >> 3) == c)
    spread_out = ones_where((r & 31) == c)
    c, lane = iota((32, 256), 0), iota((32, 256), 1)
    tile = ones_where((lane & 31) == c)
    tile_out = ones_where((lane >> 3) == c)
    r, lane = iota((256, 256), 0), iota((256, 256), 1)
    same = (r & 7) == (lane >> 5)
    same_out = (r >> 5) == (lane & 7)
    for index, w_ref in enumerate((wq_ref, wk_ref, wv_ref)):
        tall = dot(spread, w_ref[...], ((1,), (1,))).astype(BF)
        full = jnp.where(same, dot(tall, tile), 0.0)
        proj_ref[256 * index : 256 * index + 256, :] = full.astype(BF)
    tall = dot(spread_out, wo_ref[...], ((1,), (1,))).astype(BF)
    back_ref[...] = jnp.where(same_out, dot(tall, tile_out), 0.0).astype(BF)
    eye = iota((32, 32), 0) == iota((32, 32), 1)
    gains = jnp.broadcast_to(gain_ref[...], (32, 32))
    gcol = jnp.sum(jnp.where(eye, gains, 0.0), axis=1, keepdims=True)
    gcol_ref[...] = jnp.broadcast_to(gcol, (32, 128))

    r, lane = iota((256, 128), 0), iota((256, 128), 1)
    lon, base = r & 127, (r >> 7) * 64
    inner = jnp.where(lon < 16, base + 16 + lon, jnp.where(lon >= 112, base + lon - 80, -1))
    r2, lane2 = iota((32, 128), 0), iota((32, 128), 1)
    outer = jnp.where(r2 < 16, 48, 8) + (r2 & 7) + jnp.where((r2 & 8) != 0, 64, 0)
    strip_ref[...] = dot(xa_ref[2, 64:1088, 0:256], ones_where(lane == inner))
    placed = ones_where(lane2 == outer)

    to_left.wait()
    to_right.wait()
    ring = hr_ref[...].reshape(32, 1024)
    strip = strip_ref[...] + dot(ring, placed, ((0,), (0,)))
    spread_columns(xa_ref, slice(64, 1088), 2, strip.astype(BF))

    silu_layer(xa_ref, xb_ref, 0, strips)
    silu_layer(xb_ref, xc_ref, 1, strips)
    lane = iota((32, 128), 1)
    near = lane & 63
    inside = (near < 24) | (near >= 40)
    for step in range(8):
        block = chips[step]
        if step % 2 == 0:
            both = convolve(xc_ref, 2, ((block, 2), (chips[step + 1], 2)))
        strip = residual(block, 2, both[step % 2]).astype(F32)
        for m in range(2):
            for one in range(2):
                low, high = strip[64 * one : 64 * one + 32], strip[64 * one + 32 : 64 * one + 64]
                turns = [
                    pltpu.roll(part, (turn - 64 * m) % 128, 1)
                    for part, turn in ((low, -16), (low, 16), (high, 48), (high, 80))
                ]
                west = jnp.where(lane < 32, turns[0], turns[1])
                east = jnp.where(lane < 96, turns[2], turns[3])
                edge = jnp.where(lane < 64, west, east)
                main = send_ref[2 * block + one, 1, m].astype(F32)
                send_ref[2 * block + one, 1, m] = jnp.where(inside, main, edge).astype(BF)
        send_chip(1, step)

    scale = math.log2(math.e) / math.sqrt(32 // HEADS)

    def back(slot, peer):
        return pltpu.make_async_remote_copy(
            src_ref=ret_ref.at[slot, peer],
            dst_ref=got_ref.at[slot, me],
            send_sem=back_send.at[slot, peer],
            recv_sem=back_recv.at[slot, me],
            device_id={"mem": peer},
            device_id_type=MESH,
        )

    def attend(slot, carry):
        for step in (3, 2, 0, 1):
            group = order[step]
            for peer in peers_of(step):
                pltpu.make_async_remote_copy(
                    src_ref=send_ref.at[peer, slot],
                    dst_ref=recv_ref.at[slot, peer],
                    send_sem=go_send.at[slot, peer],
                    recv_sem=go_recv.at[slot, peer],
                    device_id={"mem": peer},
                    device_id_type=MESH,
                ).wait_recv()
            values = recv_ref[slot, pl.ds(4 * group, 4)].astype(F32).reshape(8, 32, 128)
            centred = values - jnp.mean(values, axis=1, keepdims=True)
            spread = jnp.mean(centred * centred, axis=1, keepdims=True)
            normed = centred * lax.rsqrt(spread + 1e-05) * gcol_ref[...][None]
            out = dot(proj_ref[...], normed.astype(BF).reshape(256, 128))
            out = out.astype(BF).astype(F32)
            q_ref[group] = (out[0:256] * scale).reshape(32, 8, 128)
            k_ref[group] = out[256:512].reshape(32, 8, 128)
            v_ref[group] = out[512:768].reshape(32, 8, 128)

        for unit in ((0, 1), (2, 3)):
            count = len(unit)

            def head(h, carry):
                queries = [[q_ref[order[i], 8 * h + d] for i in unit] for d in range(8)]

                def score(group, peak):
                    peak = list(peak)
                    for n in range(8):
                        total = [None] * count
                        for d in range(8):
                            key = k_ref[group, 8 * h + d, pl.ds(n, 8, stride=0), :]
                            for i in range(count):
                                term = queries[d][i] * key
                                total[i] = term if d == 0 else total[i] + term
                        for i in range(count):
                            s_ref[8 * group + n, i] = total[i]
                            peak[i] = jnp.maximum(peak[i], total[i])
                    return tuple(peak)

                low = jnp.full((8, 128), -jnp.inf, F32)
                peak = lax.fori_loop(0, 4, score, (low,) * count, unroll=4)

                def mix(group, state):
                    weight, mixed = list(state[0]), [list(m) for m in state[1]]
                    for n in range(8):
                        probs = [jnp.exp2(s_ref[8 * group + n, i] - peak[i]) for i in range(count)]
                        for i in range(count):
                            weight[i] = weight[i] + probs[i]
                        for d in range(8):
                            value = v_ref[group, 8 * h + d, pl.ds(n, 8, stride=0), :]
                            for i in range(count):
                                mixed[d][i] = mixed[d][i] + probs[i] * value
                    return tuple(weight), tuple(tuple(m) for m in mixed)

                zero = jnp.zeros((8, 128), F32)
                start = ((zero,) * count, ((zero,) * count,) * 8)
                weight, mixed = lax.fori_loop(0, 4, mix, start, unroll=4)
                for i in range(count):
                    inverse = 1.0 / weight[i]
                    for d in range(8):
                        mix_ref[i, 8 * h + d] = mixed[d][i] * inverse
                return carry

            lax.fori_loop(0, HEADS, head, 0)

            for i, step in enumerate(unit):
                group = order[step]
                mixed = mix_ref[i].reshape(256, 128).astype(BF)
                state = recv_ref[slot, pl.ds(4 * group, 4)].astype(F32).reshape(256, 128)
                final = dot(back_ref[...], mixed) + state
                ret_ref[slot, pl.ds(4 * group, 4)] = final.astype(BF).reshape(4, 2, 32, 128)
                if step == 3:
                    got_ref[slot, me] = ret_ref[slot, me]
                for peer in peers_of(step):
                    back(slot, peer).start()
        return carry

    lax.fori_loop(0, 2, attend, 0)

    def sent(step, carry):
        peer = lax.rem(me + step, PEERS)
        go(0, peer).wait_send()
        go(1, peer).wait_send()
        back(0, peer).wait_send()
        return carry

    lax.fori_loop(1, PEERS, sent, 0)

    lane = iota((32, 128), 1)
    middle = (lane >= 32) & (lane < 96)
    for step in range(4):
        for slot in range(2):
            for peer in peers_of(step):
                pltpu.make_async_remote_copy(
                    src_ref=ret_ref.at[slot, peer],
                    dst_ref=got_ref.at[slot, peer],
                    send_sem=back_send.at[slot, peer],
                    recv_sem=back_recv.at[slot, peer],
                    device_id={"mem": peer},
                    device_id_type=MESH,
                ).wait_recv()
        for row in range(4):
            peer = 4 * order[step] + row
            for m in range(2):
                inner, outer = got_ref[0, peer, m].astype(F32), got_ref[1, peer, m].astype(F32)
                low = jnp.where(middle, pltpu.roll(inner, 32, 1), pltpu.roll(outer, 96, 1))
                high = jnp.where(middle, pltpu.roll(inner, 96, 1), pltpu.roll(outer, 32, 1))
                z_ref[m, pl.ds(2 * peer, 32, stride=32), :] = low
                z_ref[m, pl.ds(2 * peer + 1, 32, stride=32), :] = high

    for m in range(2):
        out_ref[m] = z_ref[m].astype(BF).reshape(32, 32, 128)

    for step in range(4):
        for peer in peers_of(step):
            back(1, peer).wait_send()


def on_device(members, conv_one, conv_two, conv_three, norm_gain, w_query, w_key, w_value, w_out):
    taps = [jnp.transpose(w, (2, 3, 0, 1)) for w in (conv_one, conv_two, conv_three)]
    vmem = pl.BlockSpec(memory_space=pltpu.VMEM)
    operands = (members, *taps, norm_gain.reshape(1, 32), w_query, w_key, w_value, w_out)
    return pl.pallas_call(
        kernel,
        out_shape=jax.ShapeDtypeStruct(members.shape, BF),
        in_specs=[pl.BlockSpec(memory_space=pltpu.HBM)] * 9,
        out_specs=vmem,
        scratch_shapes=[
            pltpu.VMEM((2, 32, 32, 128), BF),
            pltpu.VMEM((5, 5, 32, 32), BF),
            pltpu.VMEM((5, 5, 32, 32), BF),
            pltpu.VMEM((5, 5, 32, 32), BF),
            pltpu.VMEM((1, 32), F32),
            pltpu.VMEM((32, 32), BF),
            pltpu.VMEM((32, 32), BF),
            pltpu.VMEM((32, 32), BF),
            pltpu.VMEM((32, 32), BF),
            pltpu.VMEM((2, 1024, 128), F32),
            pltpu.VMEM((5, 1152, 384), BF),
            pltpu.VMEM((5, 1152, 384), BF),
            pltpu.VMEM((5, 1152, 384), BF),
            pltpu.VMEM((3, 128, 1280), BF),
            pltpu.VMEM((768, 256), BF),
            pltpu.VMEM((256, 256), BF),
            pltpu.VMEM((32, 128), F32),
            pltpu.VMEM((2, 16, 1024), BF),
            pltpu.VMEM((2, 16, 1024), BF),
            pltpu.VMEM((16, 2, 2, 32, 128), BF),
            pltpu.VMEM((2, 16, 2, 32, 128), BF),
            pltpu.VMEM((4, 32, 8, 128), F32),
            pltpu.VMEM((4, 32, 8, 128), F32),
            pltpu.VMEM((4, 32, 8, 128), F32),
            pltpu.VMEM((32, 4, 8, 128), F32),
            pltpu.VMEM((4, 32, 8, 128), F32),
            pltpu.VMEM((2, 16, 2, 32, 128), BF),
            pltpu.VMEM((2, 16, 2, 32, 128), BF),
            pltpu.VMEM((1024, 128), F32),
            pltpu.SemaphoreType.DMA((2,)),
            pltpu.SemaphoreType.DMA((2,)),
            pltpu.SemaphoreType.DMA((2, 16)),
            pltpu.SemaphoreType.DMA((2, 16)),
            pltpu.SemaphoreType.DMA((2, 16)),
            pltpu.SemaphoreType.DMA((2, 16)),
            pltpu.SemaphoreType.DMA((10,)),
        ],
        compiler_params=pltpu.CompilerParams(
            collective_id=0, has_side_effects=True, vmem_limit_bytes=40 * 1024 * 1024
        ),
    )(*[pltpu.with_memory_space_constraint(value, pltpu.HBM) for value in operands])


def solution(mesh):
    in_specs = (P("mem", None, None, "lon"), P(), P(), P(), P(), P(), P(), P(), P())
    out_specs = P("mem", None, None, "lon")
    return jax.shard_map(
        on_device, mesh=mesh, in_specs=in_specs, out_specs=out_specs, check_vma=False
    )
```

```python
import math

import jax
import jax.numpy as jnp
from jax import lax
from jax.experimental import pallas as pl
from jax.experimental.pallas import tpu as pltpu
from jax.sharding import PartitionSpec as P

MESH = pl.DeviceIdType.MESH
HEADS = 4
BF = jnp.bfloat16
F32 = jnp.float32
PEERS = 16


def iota(shape, dim):
    return lax.broadcasted_iota(jnp.int32, shape, dim)


def ones_where(mask):
    return jnp.where(mask, 1.0, 0.0).astype(BF)


def dot(a, b, contract=((1,), (0,))):
    return lax.dot_general(a, b, (contract, ((), ())), preferred_element_type=F32)


def device(**where):
    return {name: index for name, index in where.items()}


def kernel(
    x_hbm,
    w1_hbm,
    w2_hbm,
    w3_hbm,
    gain_hbm,
    wq_hbm,
    wk_hbm,
    wv_hbm,
    wo_hbm,
    out_ref,
    x_ref,
    w1_ref,
    w2_ref,
    w3_ref,
    gain_ref,
    wq_ref,
    wk_ref,
    wv_ref,
    wo_ref,
    z_ref,
    xa_ref,
    xb_ref,
    xc_ref,
    band_ref,
    proj_ref,
    back_ref,
    gcol_ref,
    hs_ref,
    hr_ref,
    send_ref,
    recv_ref,
    q_ref,
    k_ref,
    v_ref,
    s_ref,
    mix_ref,
    ret_ref,
    got_ref,
    strip_ref,
    halo_send,
    halo_recv,
    go_send,
    go_recv,
    back_send,
    back_recv,
    load_sem,
):
    loads = [
        pltpu.make_async_copy(source, target, load_sem.at[index])
        for index, (source, target) in enumerate(
            (
                (x_hbm.at[0], x_ref.at[0]),
                (x_hbm.at[1], x_ref.at[1]),
                (w1_hbm, w1_ref),
                (w2_hbm, w2_ref),
                (w3_hbm, w3_ref),
                (gain_hbm, gain_ref),
                (wq_hbm, wq_ref),
                (wk_hbm, wk_ref),
                (wv_hbm, wv_ref),
                (wo_hbm, wo_ref),
            )
        )
    ]
    for load in loads:
        load.start()
    me = lax.axis_index("mem")
    col = lax.axis_index("lon")
    right, left = lax.rem(col + 1, PEERS), lax.rem(col + PEERS - 1, PEERS)

    barrier = pltpu.get_barrier_semaphore()

    def greet(step, carry):
        pl.semaphore_signal(
            barrier, inc=1, device_id={"mem": lax.rem(me + step, PEERS)}, device_id_type=MESH
        )
        return carry

    for side in (left, right):
        pl.semaphore_signal(barrier, inc=1, device_id={"lon": side}, device_id_type=MESH)
    lax.fori_loop(1, PEERS, greet, 0)

    for buf in (xa_ref, xb_ref, xc_ref):
        buf[:, 0:64, :] = jnp.zeros((5, 64, 384), BF)
        buf[:, 1088:1152, :] = jnp.zeros((5, 64, 384), BF)
    for m in range(2):
        loads[m].wait()
        z_ref[m, 0:1024, :] = x_ref[m].astype(F32).reshape(1024, 128)
        for lat in range(32):
            rows = z_ref[m, pl.ds(lat, 32, stride=32), :]
            xa_ref[2, 64 + 32 * lat : 96 + 32 * lat, 128 * m : 128 * m + 128] = rows.astype(BF)

    r, lane = iota((32, 256), 0), iota((32, 256), 1)
    want = jnp.where(r < 16, 0, 120) + (r & 7) + jnp.where((r & 8) != 0, 128, 0)
    edges = dot(ones_where(lane == want), xa_ref[2, 64:1088, 0:256], ((1,), (1,)))
    edges = edges.astype(BF)
    hs_ref[0] = edges[0:16]
    hs_ref[1] = edges[16:32]

    for load in loads[2:]:
        load.wait()

    for layer, w_ref in enumerate((w1_ref, w2_ref, w3_ref)):
        for dx in range(5):
            pieces = [w_ref[dy, dx].astype(F32) for dy in range(5)]
            base = jnp.concatenate(pieces + [jnp.zeros((32, 96), F32)], axis=1)
            for up in range(4):
                rolled = base if up == 0 else pltpu.roll(base, 32 * up, 1)
                columns = slice(256 * dx, 256 * dx + 256)
                band_ref[layer, 32 * up : 32 * up + 32, columns] = rolled.astype(BF)

    def spread_columns(target, rows, t, value):
        columns = slice(128 * t, 128 * t + 128)
        for dx in range(5):
            turned = value if dx == 2 else pltpu.roll(value, (2 - dx) % 128, 1)
            target[dx, rows, columns] = turned

    def convolve(source, layer, parts):
        windows = []
        for block, t in parts:
            rows = pl.ds(pl.multiple_of(block * 128, 128), 256)
            columns = slice(128 * t, 128 * t + 128)
            windows.append(
                jnp.concatenate([source[dx, rows, columns] for dx in range(5)], axis=0)
            )
        y = dot(band_ref[layer], jnp.concatenate(windows, axis=1))
        return [y[:, 128 * i : 128 * i + 128] for i in range(len(parts))]

    def silu_layer(source, target, layer, pieces):
        for parts in pieces:
            for (block, t), value in zip(parts, convolve(source, layer, parts)):
                value = 0.5 * value
                value = value * jnp.tanh(value) + value
                at = 64 + 128 * block
                spread_columns(target, slice(at, at + 128), t, value.astype(BF))

    own = [((block, 0), (block, 1)) for block in range(8)]
    strips = [((block, 2), (block + 1, 2)) for block in range(0, 8, 2)]

    for t in range(2):
        spread_columns(xa_ref, slice(64, 1088), t, xa_ref[2, 64:1088, 128 * t : 128 * t + 128])
    silu_layer(xa_ref, xb_ref, 0, own[:4])

    pl.semaphore_wait(barrier, PEERS + 1)

    def halo(side, target):
        return pltpu.make_async_remote_copy(
            src_ref=hs_ref.at[side],
            dst_ref=hr_ref.at[side],
            send_sem=halo_send.at[side],
            recv_sem=halo_recv.at[side],
            device_id={"lon": target},
            device_id_type=MESH,
        )

    to_left, to_right = halo(0, left), halo(1, right)
    to_left.start()
    to_right.start()

    def go(slot, peer):
        return pltpu.make_async_remote_copy(
            src_ref=send_ref.at[peer, slot],
            dst_ref=recv_ref.at[slot, me],
            send_sem=go_send.at[slot, peer],
            recv_sem=go_recv.at[slot, me],
            device_id={"mem": peer},
            device_id_type=MESH,
        )

    quarter = me // 4
    half, odd = quarter // 2, lax.rem(quarter, 2)
    order = (2 * (1 - half) + odd, 3 - 2 * half - odd, 2 * half + 1 - odd, quarter)

    def peers_of(step):
        first = 1 if step == 3 else 0
        return [4 * order[step] + lax.rem(me + row, 4) for row in range(first, 4)]

    def residual(block, t, total):
        at = pl.ds(pl.multiple_of(64 + block * 128, 64), 128)
        value = total + xa_ref[2, at, 128 * t : 128 * t + 128].astype(F32)
        return value.astype(BF)

    x_place, y_place, core = me // 8, lax.rem(me // 2, 4), lax.rem(me, 2)
    chips = [
        4 * lax.rem(x_place + across, 2) + lax.rem(y_place + along, 4)
        for across in (1, 0)
        for along in (2, 1, 3, 0)
    ]

    def send_chip(slot, step):
        if step == 7:
            recv_ref[slot, me] = send_ref[me, slot]
        else:
            go(slot, 2 * chips[step] + core).start()
        go(slot, 2 * chips[step] + 1 - core).start()

    silu_layer(xa_ref, xb_ref, 0, own[4:])
    silu_layer(xb_ref, xc_ref, 1, own)
    lane = iota((32, 128), 1)
    for step in range(8):
        block = chips[step]
        total = convolve(xc_ref, 2, ((block, 0), (block, 1)))
        for m in range(2):
            state = residual(block, m, total[m]).astype(F32)
            for one in range(2):
                low, high = state[64 * one : 64 * one + 32], state[64 * one + 32 : 64 * one + 64]
                middle = jnp.where(lane < 64, pltpu.roll(low, 96, 1), pltpu.roll(high, 32, 1))
                outer = jnp.where(lane < 64, pltpu.roll(low, 32, 1), pltpu.roll(high, 96, 1))
                send_ref[2 * block + one, 0, m] = middle.astype(BF)
                send_ref[2 * block + one, 1, m] = outer.astype(BF)
        send_chip(0, step)

    r, c = iota((256, 32), 0), iota((256, 32), 1)
    spread = ones_where((r >> 3) == c)
    spread_out = ones_where((r & 31) == c)
    c, lane = iota((32, 256), 0), iota((32, 256), 1)
    tile = ones_where((lane & 31) == c)
    tile_out = ones_where((lane >> 3) == c)
    r, lane = iota((256, 256), 0), iota((256, 256), 1)
    same = (r & 7) == (lane >> 5)
    same_out = (r >> 5) == (lane & 7)
    for index, w_ref in enumerate((wq_ref, wk_ref, wv_ref)):
        tall = dot(spread, w_ref[...], ((1,), (1,))).astype(BF)
        full = jnp.where(same, dot(tall, tile), 0.0)
        proj_ref[256 * index : 256 * index + 256, :] = full.astype(BF)
    tall = dot(spread_out, wo_ref[...], ((1,), (1,))).astype(BF)
    back_ref[...] = jnp.where(same_out, dot(tall, tile_out), 0.0).astype(BF)
    eye = iota((32, 32), 0) == iota((32, 32), 1)
    gains = jnp.broadcast_to(gain_ref[...], (32, 32))
    gcol = jnp.sum(jnp.where(eye, gains, 0.0), axis=1, keepdims=True)
    gcol_ref[...] = jnp.broadcast_to(gcol, (32, 128))

    r, lane = iota((256, 128), 0), iota((256, 128), 1)
    lon, base = r & 127, (r >> 7) * 64
    inner = jnp.where(lon < 16, base + 16 + lon, jnp.where(lon >= 112, base + lon - 80, -1))
    r2, lane2 = iota((32, 128), 0), iota((32, 128), 1)
    outer = jnp.where(r2 < 16, 48, 8) + (r2 & 7) + jnp.where((r2 & 8) != 0, 64, 0)
    strip_ref[...] = dot(xa_ref[2, 64:1088, 0:256], ones_where(lane == inner))
    placed = ones_where(lane2 == outer)

    to_left.wait()
    to_right.wait()
    ring = hr_ref[...].reshape(32, 1024)
    strip = strip_ref[...] + dot(ring, placed, ((0,), (0,)))
    spread_columns(xa_ref, slice(64, 1088), 2, strip.astype(BF))

    silu_layer(xa_ref, xb_ref, 0, strips)
    silu_layer(xb_ref, xc_ref, 1, strips)
    lane = iota((32, 128), 1)
    near = lane & 63
    inside = (near < 24) | (near >= 40)
    for step in range(8):
        block = chips[step]
        if step % 2 == 0:
            both = convolve(xc_ref, 2, ((block, 2), (chips[step + 1], 2)))
        strip = residual(block, 2, both[step % 2]).astype(F32)
        for m in range(2):
            for one in range(2):
                low, high = strip[64 * one : 64 * one + 32], strip[64 * one + 32 : 64 * one + 64]
                turns = [
                    pltpu.roll(part, (turn - 64 * m) % 128, 1)
                    for part, turn in ((low, -16), (low, 16), (high, 48), (high, 80))
                ]
                west = jnp.where(lane < 32, turns[0], turns[1])
                east = jnp.where(lane < 96, turns[2], turns[3])
                edge = jnp.where(lane < 64, west, east)
                main = send_ref[2 * block + one, 1, m].astype(F32)
                send_ref[2 * block + one, 1, m] = jnp.where(inside, main, edge).astype(BF)
        send_chip(1, step)

    scale = math.log2(math.e) / math.sqrt(32 // HEADS)

    def back(slot, peer):
        return pltpu.make_async_remote_copy(
            src_ref=ret_ref.at[slot, peer],
            dst_ref=got_ref.at[slot, me],
            send_sem=back_send.at[slot, peer],
            recv_sem=back_recv.at[slot, me],
            device_id={"mem": peer},
            device_id_type=MESH,
        )

    def attend(slot, carry):
        for step in (3, 2, 0, 1):
            group = order[step]
            for peer in peers_of(step):
                pltpu.make_async_remote_copy(
                    src_ref=send_ref.at[peer, slot],
                    dst_ref=recv_ref.at[slot, peer],
                    send_sem=go_send.at[slot, peer],
                    recv_sem=go_recv.at[slot, peer],
                    device_id={"mem": peer},
                    device_id_type=MESH,
                ).wait_recv()
            values = recv_ref[slot, pl.ds(4 * group, 4)].astype(F32).reshape(8, 32, 128)
            centred = values - jnp.mean(values, axis=1, keepdims=True)
            spread = jnp.mean(centred * centred, axis=1, keepdims=True)
            normed = centred * lax.rsqrt(spread + 1e-05) * gcol_ref[...][None]
            out = dot(proj_ref[...], normed.astype(BF).reshape(256, 128))
            out = out.astype(BF).astype(F32)
            q_ref[group] = (out[0:256] * scale).reshape(32, 8, 128)
            k_ref[group] = out[256:512].reshape(32, 8, 128)
            v_ref[group] = out[512:768].reshape(32, 8, 128)

        for unit in ((0, 1), (2, 3)):
            count = len(unit)

            def head(h, carry):
                queries = [[q_ref[order[i], 8 * h + d] for i in unit] for d in range(8)]

                def score(group, peak):
                    peak = list(peak)
                    for n in range(8):
                        total = [None] * count
                        for d in range(8):
                            key = k_ref[group, 8 * h + d, n : n + 1, :]
                            key = jnp.broadcast_to(key, (8, 128))
                            for i in range(count):
                                term = queries[d][i] * key
                                total[i] = term if d == 0 else total[i] + term
                        for i in range(count):
                            s_ref[8 * group + n, i] = total[i]
                            peak[i] = jnp.maximum(peak[i], total[i])
                    return tuple(peak)

                low = jnp.full((8, 128), -jnp.inf, F32)
                peak = lax.fori_loop(0, 4, score, (low,) * count, unroll=4)

                def mix(group, state):
                    weight, mixed = list(state[0]), [list(m) for m in state[1]]
                    for n in range(8):
                        probs = [jnp.exp2(s_ref[8 * group + n, i] - peak[i]) for i in range(count)]
                        for i in range(count):
                            weight[i] = weight[i] + probs[i]
                        for d in range(8):
                            value = v_ref[group, 8 * h + d, n : n + 1, :]
                            value = jnp.broadcast_to(value, (8, 128))
                            for i in range(count):
                                mixed[d][i] = mixed[d][i] + probs[i] * value
                    return tuple(weight), tuple(tuple(m) for m in mixed)

                zero = jnp.zeros((8, 128), F32)
                start = ((zero,) * count, ((zero,) * count,) * 8)
                weight, mixed = lax.fori_loop(0, 4, mix, start, unroll=4)
                for i in range(count):
                    inverse = 1.0 / weight[i]
                    for d in range(8):
                        mix_ref[i, 8 * h + d] = mixed[d][i] * inverse
                return carry

            lax.fori_loop(0, HEADS, head, 0)

            for i, step in enumerate(unit):
                group = order[step]
                mixed = mix_ref[i].reshape(256, 128).astype(BF)
                state = recv_ref[slot, pl.ds(4 * group, 4)].astype(F32).reshape(256, 128)
                final = dot(back_ref[...], mixed) + state
                ret_ref[slot, pl.ds(4 * group, 4)] = final.astype(BF).reshape(4, 2, 32, 128)
                if step == 3:
                    got_ref[slot, me] = ret_ref[slot, me]
                for peer in peers_of(step):
                    back(slot, peer).start()
        return carry

    lax.fori_loop(0, 2, attend, 0)

    def sent(step, carry):
        peer = lax.rem(me + step, PEERS)
        go(0, peer).wait_send()
        go(1, peer).wait_send()
        back(0, peer).wait_send()
        return carry

    lax.fori_loop(1, PEERS, sent, 0)

    lane = iota((32, 128), 1)
    middle = (lane >= 32) & (lane < 96)
    for step in range(4):
        for slot in range(2):
            for peer in peers_of(step):
                pltpu.make_async_remote_copy(
                    src_ref=ret_ref.at[slot, peer],
                    dst_ref=got_ref.at[slot, peer],
                    send_sem=back_send.at[slot, peer],
                    recv_sem=back_recv.at[slot, peer],
                    device_id={"mem": peer},
                    device_id_type=MESH,
                ).wait_recv()
        for row in range(4):
            peer = 4 * order[step] + row
            for m in range(2):
                inner, outer = got_ref[0, peer, m].astype(F32), got_ref[1, peer, m].astype(F32)
                low = jnp.where(middle, pltpu.roll(inner, 32, 1), pltpu.roll(outer, 96, 1))
                high = jnp.where(middle, pltpu.roll(inner, 96, 1), pltpu.roll(outer, 32, 1))
                z_ref[m, pl.ds(2 * peer, 32, stride=32), :] = low
                z_ref[m, pl.ds(2 * peer + 1, 32, stride=32), :] = high

    for m in range(2):
        out_ref[m] = z_ref[m, 0:1024, :].astype(BF).reshape(32, 32, 128)

    for step in range(4):
        for peer in peers_of(step):
            back(1, peer).wait_send()


def on_device(members, conv_one, conv_two, conv_three, norm_gain, w_query, w_key, w_value, w_out):
    taps = [jnp.transpose(w, (2, 3, 0, 1)) for w in (conv_one, conv_two, conv_three)]
    vmem = pl.BlockSpec(memory_space=pltpu.VMEM)
    operands = (members, *taps, norm_gain.reshape(1, 32), w_query, w_key, w_value, w_out)
    return pl.pallas_call(
        kernel,
        out_shape=jax.ShapeDtypeStruct(members.shape, BF),
        in_specs=[pl.BlockSpec(memory_space=pltpu.HBM)] * 9,
        out_specs=vmem,
        scratch_shapes=[
            pltpu.VMEM((2, 32, 32, 128), BF),
            pltpu.VMEM((5, 5, 32, 32), BF),
            pltpu.VMEM((5, 5, 32, 32), BF),
            pltpu.VMEM((5, 5, 32, 32), BF),
            pltpu.VMEM((1, 32), F32),
            pltpu.VMEM((32, 32), BF),
            pltpu.VMEM((32, 32), BF),
            pltpu.VMEM((32, 32), BF),
            pltpu.VMEM((32, 32), BF),
            pltpu.VMEM((2, 1056, 128), F32),
            pltpu.VMEM((5, 1152, 384), BF),
            pltpu.VMEM((5, 1152, 384), BF),
            pltpu.VMEM((5, 1152, 384), BF),
            pltpu.VMEM((3, 128, 1280), BF),
            pltpu.VMEM((768, 256), BF),
            pltpu.VMEM((256, 256), BF),
            pltpu.VMEM((32, 128), F32),
            pltpu.VMEM((2, 16, 1024), BF),
            pltpu.VMEM((2, 16, 1024), BF),
            pltpu.VMEM((16, 2, 2, 32, 128), BF),
            pltpu.VMEM((2, 16, 2, 32, 128), BF),
            pltpu.VMEM((4, 32, 8, 128), F32),
            pltpu.VMEM((4, 32, 8, 128), F32),
            pltpu.VMEM((4, 32, 8, 128), F32),
            pltpu.VMEM((32, 4, 8, 128), F32),
            pltpu.VMEM((4, 32, 8, 128), F32),
            pltpu.VMEM((2, 16, 2, 32, 128), BF),
            pltpu.VMEM((2, 16, 2, 32, 128), BF),
            pltpu.VMEM((1024, 128), F32),
            pltpu.SemaphoreType.DMA((2,)),
            pltpu.SemaphoreType.DMA((2,)),
            pltpu.SemaphoreType.DMA((2, 16)),
            pltpu.SemaphoreType.DMA((2, 16)),
            pltpu.SemaphoreType.DMA((2, 16)),
            pltpu.SemaphoreType.DMA((2, 16)),
            pltpu.SemaphoreType.DMA((10,)),
        ],
        compiler_params=pltpu.CompilerParams(
            collective_id=0, has_side_effects=True, vmem_limit_bytes=40 * 1024 * 1024
        ),
    )(*[pltpu.with_memory_space_constraint(value, pltpu.HBM) for value in operands])


def solution(mesh):
    in_specs = (P("mem", None, None, "lon"), P(), P(), P(), P(), P(), P(), P(), P())
    out_specs = P("mem", None, None, "lon")
    return jax.shard_map(
        on_device, mesh=mesh, in_specs=in_specs, out_specs=out_specs, check_vma=False
    )
```

```python
import math

import jax
import jax.numpy as jnp
from jax import lax
from jax.experimental import pallas as pl
from jax.experimental.pallas import tpu as pltpu
from jax.sharding import PartitionSpec as P

MESH = pl.DeviceIdType.MESH
HEADS = 4
BF = jnp.bfloat16
F32 = jnp.float32
PEERS = 16


def iota(shape, dim):
    return lax.broadcasted_iota(jnp.int32, shape, dim)


def ones_where(mask):
    return jnp.where(mask, 1.0, 0.0).astype(BF)


def dot(a, b, contract=((1,), (0,))):
    return lax.dot_general(a, b, (contract, ((), ())), preferred_element_type=F32)


def device(**where):
    return {name: index for name, index in where.items()}


def kernel(
    x_hbm,
    w1_hbm,
    w2_hbm,
    w3_hbm,
    gain_hbm,
    wq_hbm,
    wk_hbm,
    wv_hbm,
    wo_hbm,
    out_ref,
    x_ref,
    w1_ref,
    w2_ref,
    w3_ref,
    gain_ref,
    wq_ref,
    wk_ref,
    wv_ref,
    wo_ref,
    z_ref,
    xa_ref,
    xb_ref,
    xc_ref,
    band_ref,
    proj_ref,
    back_ref,
    gcol_ref,
    hs_ref,
    hr_ref,
    send_ref,
    recv_ref,
    q_ref,
    k_ref,
    v_ref,
    s_ref,
    mix_ref,
    ret_ref,
    got_ref,
    strip_ref,
    halo_send,
    halo_recv,
    go_send,
    go_recv,
    back_send,
    back_recv,
    load_sem,
):
    loads = [
        pltpu.make_async_copy(source, target, load_sem.at[index])
        for index, (source, target) in enumerate(
            (
                (x_hbm.at[0], x_ref.at[0]),
                (x_hbm.at[1], x_ref.at[1]),
                (w1_hbm, w1_ref),
                (w2_hbm, w2_ref),
                (w3_hbm, w3_ref),
                (gain_hbm, gain_ref),
                (wq_hbm, wq_ref),
                (wk_hbm, wk_ref),
                (wv_hbm, wv_ref),
                (wo_hbm, wo_ref),
            )
        )
    ]
    for load in loads:
        load.start()
    me = lax.axis_index("mem")
    col = lax.axis_index("lon")
    right, left = lax.rem(col + 1, PEERS), lax.rem(col + PEERS - 1, PEERS)

    barrier = pltpu.get_barrier_semaphore()

    def greet(step, carry):
        pl.semaphore_signal(
            barrier, inc=1, device_id={"mem": lax.rem(me + step, PEERS)}, device_id_type=MESH
        )
        return carry

    for side in (left, right):
        pl.semaphore_signal(barrier, inc=1, device_id={"lon": side}, device_id_type=MESH)
    lax.fori_loop(1, PEERS, greet, 0)

    for buf in (xa_ref, xb_ref, xc_ref):
        buf[:, 0:64, :] = jnp.zeros((5, 64, 384), BF)
        buf[:, 1088:1152, :] = jnp.zeros((5, 64, 384), BF)
    for m in range(2):
        loads[m].wait()
        z_ref[m, 0:1024, :] = x_ref[m].astype(F32).reshape(1024, 128)
        for lat in range(32):
            rows = z_ref[m, pl.ds(lat, 32, stride=32), :]
            xa_ref[2, 64 + 32 * lat : 96 + 32 * lat, 128 * m : 128 * m + 128] = rows.astype(BF)

    r, lane = iota((32, 256), 0), iota((32, 256), 1)
    want = jnp.where(r < 16, 0, 120) + (r & 7) + jnp.where((r & 8) != 0, 128, 0)
    edges = dot(ones_where(lane == want), xa_ref[2, 64:1088, 0:256], ((1,), (1,)))
    edges = edges.astype(BF)
    hs_ref[0] = edges[0:16]
    hs_ref[1] = edges[16:32]

    for load in loads[2:]:
        load.wait()

    for layer, w_ref in enumerate((w1_ref, w2_ref, w3_ref)):
        for dx in range(5):
            pieces = [w_ref[dy, dx].astype(F32) for dy in range(5)]
            base = jnp.concatenate(pieces + [jnp.zeros((32, 96), F32)], axis=1)
            for up in range(4):
                rolled = base if up == 0 else pltpu.roll(base, 32 * up, 1)
                columns = slice(256 * dx, 256 * dx + 256)
                band_ref[layer, 32 * up : 32 * up + 32, columns] = rolled.astype(BF)

    def spread_columns(target, rows, t, value):
        columns = slice(128 * t, 128 * t + 128)
        for dx in range(5):
            turned = value if dx == 2 else pltpu.roll(value, (2 - dx) % 128, 1)
            target[dx, rows, columns] = turned

    def convolve(source, layer, parts):
        windows = []
        for block, t in parts:
            rows = pl.ds(pl.multiple_of(block * 128, 128), 256)
            columns = slice(128 * t, 128 * t + 128)
            windows.append(
                jnp.concatenate([source[dx, rows, columns] for dx in range(5)], axis=0)
            )
        y = dot(band_ref[layer], jnp.concatenate(windows, axis=1))
        return [y[:, 128 * i : 128 * i + 128] for i in range(len(parts))]

    def silu_layer(source, target, layer, pieces):
        for parts in pieces:
            for (block, t), value in zip(parts, convolve(source, layer, parts)):
                value = 0.5 * value
                value = value * jnp.tanh(value) + value
                at = 64 + 128 * block
                spread_columns(target, slice(at, at + 128), t, value.astype(BF))

    own = [((block, 0), (block, 1)) for block in range(8)]
    strips = [((block, 2), (block + 1, 2)) for block in range(0, 8, 2)]

    for t in range(2):
        spread_columns(xa_ref, slice(64, 1088), t, xa_ref[2, 64:1088, 128 * t : 128 * t + 128])
    silu_layer(xa_ref, xb_ref, 0, own[:4])

    pl.semaphore_wait(barrier, PEERS + 1)

    def halo(side, target):
        return pltpu.make_async_remote_copy(
            src_ref=hs_ref.at[side],
            dst_ref=hr_ref.at[side],
            send_sem=halo_send.at[side],
            recv_sem=halo_recv.at[side],
            device_id={"lon": target},
            device_id_type=MESH,
        )

    to_left, to_right = halo(0, left), halo(1, right)
    to_left.start()
    to_right.start()

    def go(slot, peer):
        return pltpu.make_async_remote_copy(
            src_ref=send_ref.at[peer, slot],
            dst_ref=recv_ref.at[slot, me],
            send_sem=go_send.at[slot, peer],
            recv_sem=go_recv.at[slot, me],
            device_id={"mem": peer},
            device_id_type=MESH,
        )

    quarter = me // 4
    half, odd = quarter // 2, lax.rem(quarter, 2)
    order = (2 * (1 - half) + odd, 3 - 2 * half - odd, 2 * half + 1 - odd, quarter)

    def peers_of(step):
        first = 1 if step == 3 else 0
        return [4 * order[step] + lax.rem(me + row, 4) for row in range(first, 4)]

    def residual(block, t, total):
        at = pl.ds(pl.multiple_of(64 + block * 128, 64), 128)
        value = total + xa_ref[2, at, 128 * t : 128 * t + 128].astype(F32)
        return value.astype(BF)

    x_place, y_place, core = me // 8, lax.rem(me // 2, 4), lax.rem(me, 2)
    chips = [
        4 * lax.rem(x_place + across, 2) + lax.rem(y_place + along, 4)
        for across in (1, 0)
        for along in (2, 1, 3, 0)
    ]

    def send_chip(slot, step):
        if step == 7:
            recv_ref[slot, me] = send_ref[me, slot]
        else:
            go(slot, 2 * chips[step] + core).start()
        go(slot, 2 * chips[step] + 1 - core).start()

    silu_layer(xa_ref, xb_ref, 0, own[4:])
    silu_layer(xb_ref, xc_ref, 1, own)
    lane = iota((32, 128), 1)
    for step in range(8):
        block = chips[step]
        total = convolve(xc_ref, 2, ((block, 0), (block, 1)))
        for m in range(2):
            state = residual(block, m, total[m]).astype(F32)
            for one in range(2):
                low, high = state[64 * one : 64 * one + 32], state[64 * one + 32 : 64 * one + 64]
                middle = jnp.where(lane < 64, pltpu.roll(low, 96, 1), pltpu.roll(high, 32, 1))
                outer = jnp.where(lane < 64, pltpu.roll(low, 32, 1), pltpu.roll(high, 96, 1))
                send_ref[2 * block + one, 0, m] = middle.astype(BF)
                send_ref[2 * block + one, 1, m] = outer.astype(BF)
        send_chip(0, step)

    r, c = iota((256, 32), 0), iota((256, 32), 1)
    spread = ones_where((r >> 3) == c)
    spread_out = ones_where((r & 31) == c)
    c, lane = iota((32, 256), 0), iota((32, 256), 1)
    tile = ones_where((lane & 31) == c)
    tile_out = ones_where((lane >> 3) == c)
    r, lane = iota((256, 256), 0), iota((256, 256), 1)
    same = (r & 7) == (lane >> 5)
    same_out = (r >> 5) == (lane & 7)
    for index, w_ref in enumerate((wq_ref, wk_ref, wv_ref)):
        tall = dot(spread, w_ref[...], ((1,), (1,))).astype(BF)
        full = jnp.where(same, dot(tall, tile), 0.0)
        proj_ref[256 * index : 256 * index + 256, :] = full.astype(BF)
    tall = dot(spread_out, wo_ref[...], ((1,), (1,))).astype(BF)
    back_ref[...] = jnp.where(same_out, dot(tall, tile_out), 0.0).astype(BF)
    eye = iota((32, 32), 0) == iota((32, 32), 1)
    gains = jnp.broadcast_to(gain_ref[...], (32, 32))
    gcol = jnp.sum(jnp.where(eye, gains, 0.0), axis=1, keepdims=True)
    gcol_ref[...] = jnp.broadcast_to(gcol, (32, 128))

    r, lane = iota((256, 128), 0), iota((256, 128), 1)
    lon, base = r & 127, (r >> 7) * 64
    inner = jnp.where(lon < 16, base + 16 + lon, jnp.where(lon >= 112, base + lon - 80, -1))
    r2, lane2 = iota((32, 128), 0), iota((32, 128), 1)
    outer = jnp.where(r2 < 16, 48, 8) + (r2 & 7) + jnp.where((r2 & 8) != 0, 64, 0)
    strip_ref[...] = dot(xa_ref[2, 64:1088, 0:256], ones_where(lane == inner))
    placed = ones_where(lane2 == outer)

    to_left.wait()
    to_right.wait()
    ring = hr_ref[...].reshape(32, 1024)
    strip = strip_ref[...] + dot(ring, placed, ((0,), (0,)))
    spread_columns(xa_ref, slice(64, 1088), 2, strip.astype(BF))

    silu_layer(xa_ref, xb_ref, 0, strips)
    silu_layer(xb_ref, xc_ref, 1, strips)
    lane = iota((32, 128), 1)
    near = lane & 63
    inside = (near < 24) | (near >= 40)
    for step in range(8):
        block = chips[step]
        if step % 2 == 0:
            both = convolve(xc_ref, 2, ((block, 2), (chips[step + 1], 2)))
        strip = residual(block, 2, both[step % 2]).astype(F32)
        for m in range(2):
            for one in range(2):
                low, high = strip[64 * one : 64 * one + 32], strip[64 * one + 32 : 64 * one + 64]
                turns = [
                    pltpu.roll(part, (turn - 64 * m) % 128, 1)
                    for part, turn in ((low, -16), (low, 16), (high, 48), (high, 80))
                ]
                west = jnp.where(lane < 32, turns[0], turns[1])
                east = jnp.where(lane < 96, turns[2], turns[3])
                edge = jnp.where(lane < 64, west, east)
                main = send_ref[2 * block + one, 1, m].astype(F32)
                send_ref[2 * block + one, 1, m] = jnp.where(inside, main, edge).astype(BF)
        send_chip(1, step)

    scale = math.log2(math.e) / math.sqrt(32 // HEADS)

    def back(slot, peer):
        return pltpu.make_async_remote_copy(
            src_ref=ret_ref.at[slot, peer],
            dst_ref=got_ref.at[slot, me],
            send_sem=back_send.at[slot, peer],
            recv_sem=back_recv.at[slot, me],
            device_id={"mem": peer},
            device_id_type=MESH,
        )

    def attend(slot, units):
        for step in (3, 2, 0, 1):
            group = order[step]
            for peer in peers_of(step):
                pltpu.make_async_remote_copy(
                    src_ref=send_ref.at[peer, slot],
                    dst_ref=recv_ref.at[slot, peer],
                    send_sem=go_send.at[slot, peer],
                    recv_sem=go_recv.at[slot, peer],
                    device_id={"mem": peer},
                    device_id_type=MESH,
                ).wait_recv()
            values = recv_ref[slot, pl.ds(4 * group, 4)].astype(F32).reshape(8, 32, 128)
            centred = values - jnp.mean(values, axis=1, keepdims=True)
            spread = jnp.mean(centred * centred, axis=1, keepdims=True)
            normed = centred * lax.rsqrt(spread + 1e-05) * gcol_ref[...][None]
            out = dot(proj_ref[...], normed.astype(BF).reshape(256, 128))
            out = out.astype(BF).astype(F32)
            q_ref[group] = (out[0:256] * scale).reshape(32, 8, 128)
            k_ref[group] = out[256:512].reshape(32, 8, 128)
            v_ref[group] = out[512:768].reshape(32, 8, 128)

        for unit in units:
            count = len(unit)

            def head(h, carry):
                queries = [[q_ref[order[i], 8 * h + d] for i in unit] for d in range(8)]

                def score(group, peak):
                    peak = list(peak)
                    for n in range(8):
                        total = [None] * count
                        for d in range(8):
                            key = k_ref[group, 8 * h + d, n : n + 1, :]
                            key = jnp.broadcast_to(key, (8, 128))
                            for i in range(count):
                                term = queries[d][i] * key
                                total[i] = term if d == 0 else total[i] + term
                        for i in range(count):
                            s_ref[8 * group + n, i] = total[i]
                            peak[i] = jnp.maximum(peak[i], total[i])
                    return tuple(peak)

                low = jnp.full((8, 128), -jnp.inf, F32)
                peak = lax.fori_loop(0, 4, score, (low,) * count, unroll=4)

                def mix(group, state):
                    weight, mixed = list(state[0]), [list(m) for m in state[1]]
                    for n in range(8):
                        probs = [jnp.exp2(s_ref[8 * group + n, i] - peak[i]) for i in range(count)]
                        for i in range(count):
                            weight[i] = weight[i] + probs[i]
                        for d in range(8):
                            value = v_ref[group, 8 * h + d, n : n + 1, :]
                            value = jnp.broadcast_to(value, (8, 128))
                            for i in range(count):
                                mixed[d][i] = mixed[d][i] + probs[i] * value
                    return tuple(weight), tuple(tuple(m) for m in mixed)

                zero = jnp.zeros((8, 128), F32)
                start = ((zero,) * count, ((zero,) * count,) * 8)
                weight, mixed = lax.fori_loop(0, 4, mix, start, unroll=4)
                for i in range(count):
                    inverse = 1.0 / weight[i]
                    for d in range(8):
                        mix_ref[i, 8 * h + d] = mixed[d][i] * inverse
                return carry

            lax.fori_loop(0, HEADS, head, 0)

            for i, step in enumerate(unit):
                group = order[step]
                mixed = mix_ref[i].reshape(256, 128).astype(BF)
                state = recv_ref[slot, pl.ds(4 * group, 4)].astype(F32).reshape(256, 128)
                final = dot(back_ref[...], mixed) + state
                ret_ref[slot, pl.ds(4 * group, 4)] = final.astype(BF).reshape(4, 2, 32, 128)
                if step == 3:
                    got_ref[slot, me] = ret_ref[slot, me]
                for peer in peers_of(step):
                    back(slot, peer).start()

    attend(0, ((0, 1), (2, 3)))
    attend(1, ((0, 1), (2,), (3,)))

    def sent(step, carry):
        peer = lax.rem(me + step, PEERS)
        go(0, peer).wait_send()
        go(1, peer).wait_send()
        back(0, peer).wait_send()
        return carry

    lax.fori_loop(1, PEERS, sent, 0)

    lane = iota((32, 128), 1)
    middle = (lane >= 32) & (lane < 96)
    for step in range(4):
        for slot in range(2):
            for peer in peers_of(step):
                pltpu.make_async_remote_copy(
                    src_ref=ret_ref.at[slot, peer],
                    dst_ref=got_ref.at[slot, peer],
                    send_sem=back_send.at[slot, peer],
                    recv_sem=back_recv.at[slot, peer],
                    device_id={"mem": peer},
                    device_id_type=MESH,
                ).wait_recv()
        for row in range(4):
            peer = 4 * order[step] + row
            for m in range(2):
                inner, outer = got_ref[0, peer, m].astype(F32), got_ref[1, peer, m].astype(F32)
                low = jnp.where(middle, pltpu.roll(inner, 32, 1), pltpu.roll(outer, 96, 1))
                high = jnp.where(middle, pltpu.roll(inner, 96, 1), pltpu.roll(outer, 32, 1))
                z_ref[m, pl.ds(2 * peer, 32, stride=32), :] = low
                z_ref[m, pl.ds(2 * peer + 1, 32, stride=32), :] = high

    for m in range(2):
        out_ref[m] = z_ref[m, 0:1024, :].astype(BF).reshape(32, 32, 128)

    for step in range(4):
        for peer in peers_of(step):
            back(1, peer).wait_send()


def on_device(members, conv_one, conv_two, conv_three, norm_gain, w_query, w_key, w_value, w_out):
    taps = [jnp.transpose(w, (2, 3, 0, 1)) for w in (conv_one, conv_two, conv_three)]
    vmem = pl.BlockSpec(memory_space=pltpu.VMEM)
    operands = (members, *taps, norm_gain.reshape(1, 32), w_query, w_key, w_value, w_out)
    return pl.pallas_call(
        kernel,
        out_shape=jax.ShapeDtypeStruct(members.shape, BF),
        in_specs=[pl.BlockSpec(memory_space=pltpu.HBM)] * 9,
        out_specs=vmem,
        scratch_shapes=[
            pltpu.VMEM((2, 32, 32, 128), BF),
            pltpu.VMEM((5, 5, 32, 32), BF),
            pltpu.VMEM((5, 5, 32, 32), BF),
            pltpu.VMEM((5, 5, 32, 32), BF),
            pltpu.VMEM((1, 32), F32),
            pltpu.VMEM((32, 32), BF),
            pltpu.VMEM((32, 32), BF),
            pltpu.VMEM((32, 32), BF),
            pltpu.VMEM((32, 32), BF),
            pltpu.VMEM((2, 1056, 128), F32),
            pltpu.VMEM((5, 1152, 384), BF),
            pltpu.VMEM((5, 1152, 384), BF),
            pltpu.VMEM((5, 1152, 384), BF),
            pltpu.VMEM((3, 128, 1280), BF),
            pltpu.VMEM((768, 256), BF),
            pltpu.VMEM((256, 256), BF),
            pltpu.VMEM((32, 128), F32),
            pltpu.VMEM((2, 16, 1024), BF),
            pltpu.VMEM((2, 16, 1024), BF),
            pltpu.VMEM((16, 2, 2, 32, 128), BF),
            pltpu.VMEM((2, 16, 2, 32, 128), BF),
            pltpu.VMEM((4, 32, 8, 128), F32),
            pltpu.VMEM((4, 32, 8, 128), F32),
            pltpu.VMEM((4, 32, 8, 128), F32),
            pltpu.VMEM((32, 4, 8, 128), F32),
            pltpu.VMEM((4, 32, 8, 128), F32),
            pltpu.VMEM((2, 16, 2, 32, 128), BF),
            pltpu.VMEM((2, 16, 2, 32, 128), BF),
            pltpu.VMEM((1024, 128), F32),
            pltpu.SemaphoreType.DMA((2,)),
            pltpu.SemaphoreType.DMA((2,)),
            pltpu.SemaphoreType.DMA((2, 16)),
            pltpu.SemaphoreType.DMA((2, 16)),
            pltpu.SemaphoreType.DMA((2, 16)),
            pltpu.SemaphoreType.DMA((2, 16)),
            pltpu.SemaphoreType.DMA((10,)),
        ],
        compiler_params=pltpu.CompilerParams(
            collective_id=0, has_side_effects=True, vmem_limit_bytes=40 * 1024 * 1024
        ),
    )(*[pltpu.with_memory_space_constraint(value, pltpu.HBM) for value in operands])


def solution(mesh):
    in_specs = (P("mem", None, None, "lon"), P(), P(), P(), P(), P(), P(), P(), P())
    out_specs = P("mem", None, None, "lon")
    return jax.shard_map(
        on_device, mesh=mesh, in_specs=in_specs, out_specs=out_specs, check_vma=False
    )
```
